32 devices in a mesh: dp: 2 (over x), expert: 16 (over z, y, core).
Axes of the slice: x: 2, y: 2, z: 4, core: 2. Of those that a mesh axis runs over, the one named last changes fastest.
Arguments:
- tokens: bfloat16 [4096, 2048], P(('dp', 'expert')), may hold values from -6 to 6
- out_grad: bfloat16 [4096, 2048], P(('dp', 'expert')), may hold values from -6 to 6
- route_gates: float32 [4096, 2], P(('dp', 'expert')), may hold values from 0.1 to 1
- route_slot: int32 [4096, 2], P(('dp', 'expert')), may hold values from 0 to 15, all different within a row; in each aligned block of 128 rows (0 to 127, 128 to 255, ...) at most 20 rows name the same one
- gate_weight: bfloat16 [16, 2048, 768], P('expert', 'dp'), may hold values from -0.125 to 0.125
- up_weight: bfloat16 [16, 2048, 768], P('expert', 'dp'), may hold values from -0.125 to 0.125
- down_weight: bfloat16 [16, 2048, 768], P('expert', 'dp'), may hold values from -0.21875 to 0.21875
Outputs:
- moe_out: bfloat16 [4096, 2048], P(('dp', 'expert'))
- token_grad: bfloat16 [4096, 2048], P(('dp', 'expert'))
- down_grad: bfloat16 [16, 2048, 768], P('expert', 'dp')
The draws below stay inside these ranges and needn't reach their ends.
Inputs may be any that keep to these rules, and one draw needn't show every extreme that they name: `route_slot`: the 2 routes of a token name different slots. At most 20 routes of the tokens of one device name one slot, and in every draw some device sends exactly 20 routes to some slot.
All inputs are finite; a program needn't handle non-finite values.
Results may differ from the reference program's by a relative error of at most 0.014.
Values may be sent and summed in bfloat16 or wider, within the bound.
No kernel may reach another device: no remote copies, remote signals or barrier semaphores. Data moves between devices by JAX's collectives and lax.ppermute only.
A program may use at most 64 MiB of HBM per device.

```python
import math
import jax
import jax.numpy as jnp
import numpy as np
from jax import lax

D = 2048
FF = 768
TOPK = 2
TOK_DEV = 128
SLOTS = 16
CAP = 20
TOKENS = 4096
N_DP = 2
N_EXPERT = 16


def steps_of(rng, dims, pieces, least, largest):
    gain, own = 1.0, jax.random.fold_in(rng, 6)
    for dim, blocks in pieces:
        heights = jnp.exp(jax.random.uniform(jax.random.fold_in(own, dim), (blocks,), jnp.float32, least / len(pieces), largest / len(pieces)))
        gain = gain * jnp.repeat(heights, dims[dim] // blocks).reshape([-1 if axis == dim else 1 for axis in range(len(dims))])
    return gain


def deal_out(rng, own, number, rows, count, top, bound, skew):
    sequence = jax.random.permutation(rng, count)
    heavy_load, usual = shares(count, rows * top, bound, skew, True), shares(count, rows * top, bound, skew, False)
    places = jnp.arange(count)

    def named(lengths, offset_by):
        used = int((lengths > 0).sum())
        fixed = max(1, used // 4)
        shifted = fixed + (places - fixed + offset_by * (used - fixed)) % max(1, count - fixed)
        return jnp.zeros((count,), jnp.int32).at[sequence[jnp.where(places < fixed, places, shifted)]].set(jnp.asarray(lengths, jnp.int32))

    lengths = jnp.where(number % 4 == 0, named(heavy_load, number // 4), named(usual, number - number // 4 - 1))
    mixed = jax.random.permutation(jax.random.fold_in(own, 3), count)
    source_of, taker = mixed[0:count // 2 * 2:2], mixed[1:count // 2 * 2:2]
    slack = jnp.minimum(lengths[source_of] - 1, bound - lengths[taker]) // 2
    slack = jnp.where((source_of == sequence[0]) | (taker == sequence[0]) | (lengths[taker] == 0), 0, jnp.maximum(slack, 0))
    shifted = jax.random.randint(jax.random.fold_in(own, 4), (count // 2,), 0, 1 << 20) % (slack + 1)
    lengths = lengths.at[source_of].add(-shifted).at[taker].add(shifted)
    labels = jnp.searchsorted(jnp.cumsum(lengths), jnp.arange(rows * top), side="right").astype(jnp.int32)
    grid = labels.reshape(top, rows).T
    grid = grid[jax.random.permutation(jax.random.fold_in(own, 1), rows)]
    offset_by = jax.random.randint(jax.random.fold_in(own, 2), (rows, 1), 0, top)
    return jnp.take_along_axis(grid, (jnp.arange(top)[None, :] + offset_by) % top, axis=1)


def shares(number_of, total, bound, skew, full):
    weights = [(1 << 20) // math.isqrt(rank ** skew) + 1 for rank in range(1, number_of + 1)]
    largest = bound if full else min(bound, max(-(-total // number_of), total * weights[0] // sum(weights)))
    least = 1 if total - largest >= number_of - 1 else 0
    holding, spare = [largest] + [least] * (number_of - 1), total - largest - least * (number_of - 1)
    while spare > 0:
        candidates = [i for i in range(1, number_of) if holding[i] < largest] or [i for i in range(1, number_of) if holding[i] < bound]
        mass, budget = sum([weights[i] for i in candidates]), spare
        for i in candidates:
            extra = min(bound - holding[i], max(1, budget * weights[i] // mass), spare)
            holding[i] = holding[i] + extra
            spare = spare - extra
    return np.array(holding)


def normal_values(rng, shape, deviation, limit, cuts=(), held_as=jnp.bfloat16):
    result = deviation * jax.random.normal(rng, shape, jnp.float32)
    if cuts:
        result = result * steps_of(rng, shape, cuts, -0.22, 0.18)
    return jnp.clip(result, -limit, limit).astype(held_as)


def setup_inputs(seed: int = 0) -> dict:
    key_list = jax.random.split(jax.random.key(seed), 8)
    tokens = normal_values(key_list[0], (TOKENS, D), 1.0, 6.0, ((0, 32),))
    out_grad = normal_values(key_list[1], (TOKENS, D), 1.0, 6.0, ((0, 32),))
    route_gates = jnp.clip(0.1 + 0.9 * jax.random.uniform(key_list[2], (TOKENS, TOPK), jnp.float32) ** steps_of(key_list[2], (TOKENS, TOPK), ((0, 32),), -0.2, 0.2), 0.1, 1.0)
    route_slot_keys = jax.random.split(jax.random.fold_in(key_list[3], 1), TOKENS // TOK_DEV)
    route_slot_turns = jax.random.permutation(jax.random.fold_in(key_list[3], 3), TOKENS // TOK_DEV)
    route_slot = jax.vmap(lambda own, number: deal_out(jax.random.fold_in(key_list[3], 2), own, number, TOK_DEV, SLOTS, TOPK, CAP, 2))(route_slot_keys, route_slot_turns).reshape((TOKENS, TOPK))
    gate_weight = normal_values(key_list[4], (SLOTS, D, FF), D ** -0.5, 0.125, ((0, 16), (1, 2)))
    up_weight = normal_values(key_list[5], (SLOTS, D, FF), D ** -0.5, 0.125, ((0, 16), (1, 2)))
    down_weight = normal_values(key_list[6], (SLOTS, D, FF), FF ** -0.5, 0.21875, ((0, 16), (1, 2)))
    return dict(tokens=tokens, out_grad=out_grad, route_gates=route_gates, route_slot=route_slot, gate_weight=gate_weight, up_weight=up_weight, down_weight=down_weight)


def silu_parts(gate_proj):
    sigma_gate = jax.nn.sigmoid(gate_proj)
    return gate_proj * sigma_gate, sigma_gate


def reference(tokens, out_grad, route_gates, route_slot, gate_weight, up_weight, down_weight):
    route_total = TOK_DEV * TOPK
    buffer_rows = N_EXPERT * CAP
    all_routes = N_DP * N_EXPERT * route_total
    routes_dev = route_slot.reshape(N_DP, N_EXPERT, route_total).astype(jnp.int32)
    slot_ids = jnp.arange(SLOTS, dtype=jnp.int32)
    onehot = (routes_dev[:, :, :, None] == slot_ids[None, None, None, :]).astype(jnp.int32)
    slot_rank = jnp.sum((jnp.cumsum(onehot, axis=2) - onehot) * onehot, axis=3).astype(jnp.int32)
    group_index = jnp.broadcast_to(jnp.arange(N_DP, dtype=jnp.int32)[:, None, None], routes_dev.shape)
    source_index = jnp.broadcast_to(jnp.arange(N_EXPERT, dtype=jnp.int32)[None, :, None], routes_dev.shape)
    route_index = ((group_index * N_EXPERT + source_index) * route_total
                   + jnp.arange(route_total, dtype=jnp.int32)[None, None, :]).astype(jnp.int32)
    route_table = jnp.full((N_DP, SLOTS, buffer_rows), all_routes, jnp.int32)
    route_table = route_table.at[group_index, routes_dev, (source_index * CAP + slot_rank).astype(jnp.int32)].set(route_index)
    route_table = jnp.transpose(route_table, (1, 0, 2))
    gates_flat = route_gates.reshape(-1)

    def per_slot(totals, inputs):
        out_sum, grad_sum = totals
        index_rows, w_gate, w_up, w_down = inputs
        filled = index_rows < all_routes
        safe_index = jnp.where(filled, index_rows, 0).astype(jnp.int32)
        token_index = (safe_index // TOPK).astype(jnp.int32)
        gate_value = jnp.where(filled, gates_flat[safe_index], jnp.zeros((), gates_flat.dtype))
        rows_in = jnp.where(filled[:, :, None], tokens[token_index], jnp.zeros((), tokens.dtype)).reshape(-1, D)
        rows_grad = (gate_value[:, :, None] * out_grad[token_index].astype(jnp.float32)).astype(jnp.bfloat16).reshape(-1, D)
        gate_proj = jnp.dot(rows_in, w_gate, preferred_element_type=jnp.float32)
        up_proj = jnp.dot(rows_in, w_up, preferred_element_type=jnp.float32)
        activated, sigma_gate = silu_parts(gate_proj)
        hidden = (activated * up_proj).astype(jnp.bfloat16)
        outputs = jnp.dot(hidden, w_down.T, preferred_element_type=jnp.float32).astype(jnp.bfloat16)
        grad_hidden = jnp.dot(rows_grad, w_down, preferred_element_type=jnp.float32)
        grad_gate = (grad_hidden * up_proj * sigma_gate * (1.0 + gate_proj * (1.0 - sigma_gate))).astype(jnp.bfloat16)
        grad_up = (grad_hidden * activated).astype(jnp.bfloat16)
        grad_rows = (jnp.dot(grad_gate, w_gate.T, preferred_element_type=jnp.float32)
                     + jnp.dot(grad_up, w_up.T, preferred_element_type=jnp.float32)).astype(jnp.bfloat16)
        group_parts = jnp.einsum("grd,grf->gdf",
                                 rows_grad.reshape(N_DP, buffer_rows, D).astype(jnp.float32),
                                 hidden.reshape(N_DP, buffer_rows, FF).astype(jnp.float32)).astype(jnp.bfloat16)
        down_slot = jnp.sum(group_parts.astype(jnp.float32), axis=0).astype(jnp.bfloat16)
        target_rows = jnp.where(filled, token_index, TOKENS).reshape(-1).astype(jnp.int32)
        out_sum = out_sum.at[target_rows].add(gate_value.reshape(-1)[:, None] * outputs.astype(jnp.float32), mode="drop")
        grad_sum = grad_sum.at[target_rows].add(grad_rows.astype(jnp.float32), mode="drop")
        return (out_sum, grad_sum), down_slot

    start_sums = (jnp.zeros((TOKENS, D), jnp.float32), jnp.zeros((TOKENS, D), jnp.float32))
    (out_sum, grad_sum), down_grad = lax.scan(per_slot, start_sums, (route_table, gate_weight, up_weight, down_weight))
    return out_sum.astype(jnp.bfloat16), grad_sum.astype(jnp.bfloat16), down_grad
```

```python
import functools

import jax
import jax.numpy as jnp
from jax import lax
from jax.experimental import pallas as pl
from jax.experimental.pallas import tpu as pltpu
from jax.sharding import PartitionSpec as P

F32, BF16, I32 = jnp.float32, jnp.bfloat16, jnp.int32
NT = (((1,), (1,)), ((), ()))
TN = (((0,), (0,)), ((), ()))


def mm(a, b, dims=(((1,), (0,)), ((), ()))):
    return lax.dot_general(a, b, dims, preferred_element_type=F32)


def ones_where(mask):
    return jnp.where(mask, 1.0, 0.0).astype(BF16)


def iota(shape, dim):
    return lax.broadcasted_iota(I32, shape, dim)


def call(kernel, out_shape, grid, in_specs, out_specs, scratch=(), flops=0, moved=0, vmem_mib=28):
    return pl.pallas_call(
        kernel,
        out_shape=out_shape,
        grid=grid,
        in_specs=in_specs,
        out_specs=out_specs,
        scratch_shapes=list(scratch),
        cost_estimate=pl.CostEstimate(flops=flops, bytes_accessed=moved, transcendentals=0),
        compiler_params=pltpu.CompilerParams(vmem_limit_bytes=vmem_mib * 2**20),
    )


def whole(shape):
    return pl.BlockSpec(shape, lambda *_: (0,) * len(shape))


SCALAR = pl.BlockSpec(memory_space=pltpu.SMEM)


def places_in_lanes(slots, peers, cap):
    top, count = slots.shape
    named = [jnp.where(iota((peers, count), 0) == slots[k : k + 1, :], 1.0, 0.0) for k in range(top)]
    earlier = ones_where(iota((count, count), 0) < iota((count, count), 1))
    before = mm(sum(named).astype(BF16), earlier)
    ranks = [jnp.sum(before * each, axis=0, keepdims=True).astype(I32) for each in named]
    return [slots[k : k + 1, :] * (2 * cap) + ranks[k] for k in range(top)]


def places_in_rows(slots, peers, cap):
    count, top = slots.shape
    named = [jnp.where(iota((count, peers), 1) == slots[:, k : k + 1], 1.0, 0.0) for k in range(top)]
    earlier = ones_where(iota((count, count), 1) < iota((count, count), 0))
    before = mm(earlier, sum(named).astype(BF16))
    ranks = [jnp.sum(before * each, axis=1, keepdims=True).astype(I32) for each in named]
    return [slots[:, k : k + 1] * (2 * cap) + ranks[k] for k in range(top)]


def send_tokens_kernel(peers, cap, slots_ref, tok_ref, out_ref):
    places = places_in_lanes(slots_ref[...], peers, cap)
    rows, count = 2 * cap * peers, slots_ref.shape[1]
    at = iota((rows, count), 0)
    halves = [sum(jnp.where(at == place + h * cap, 1.0, 0.0) for place in places) for h in range(2)]
    pick = jnp.concatenate(halves, axis=1).astype(BF16)
    width = out_ref.shape[2]
    for part in range(2):
        lo = part * 2 * width
        both = jnp.concatenate(
            [tok_ref[:, lo : lo + width], tok_ref[:, lo + width : lo + 2 * width]], axis=0
        )
        out_ref[part] = mm(pick, both).astype(BF16)


def send_grads_kernel(peers, cap, slots_ref, gates_ref, grad_ref, out_ref):
    places = places_in_lanes(slots_ref[...], peers, cap)
    rows, count = 2 * cap * peers, slots_ref.shape[1]
    half = out_ref.shape[1]
    at = iota((rows, count), 0)
    gates = gates_ref[...]
    picks = [
        jnp.concatenate([jnp.where(at == place + h * cap, 1.0, 0.0) for h in range(2)], axis=1).astype(BF16)
        for place in places
    ]
    step = min(512, half)
    for lo in range(0, half, step):
        total = None
        for k, pick in enumerate(picks):
            both = jnp.concatenate(
                [
                    (gates[:, k : k + 1] * grad_ref[:, c : c + step].astype(F32)).astype(BF16)
                    for c in (lo, half + lo)
                ],
                axis=0,
            )
            rows_k = mm(pick, both)
            total = rows_k if total is None else total + rows_k
        out_ref[:, lo : lo + step] = total.astype(BF16)


def partial_kernel(group_ref, target_ref, recv_ref, wg_ref, wu_ref, gate_ref, up_ref, send_ref, x_ref):
    rows = gate_ref.shape[0]
    width = recv_ref.shape[2]

    @pl.when(pl.program_id(0) == 0)
    def _():
        pick = ones_where(iota((2 * rows, 2 * rows), 1) == target_ref[...])
        for part in range(2):
            for h in range(2):
                x_ref[part * rows : (part + 1) * rows, h * width : (h + 1) * width] = mm(
                    pick[h * rows : (h + 1) * rows], recv_ref[part]
                ).astype(BF16)

    group = group_ref[0]
    mine = x_ref[pl.ds(pl.multiple_of(group * rows, 16), rows), :]
    other = x_ref[pl.ds(pl.multiple_of((1 - group) * rows, 16), rows), :]
    wg, wu = wg_ref[...], wu_ref[...]
    send_ref[0] = mm(other, wg).astype(BF16)
    send_ref[1] = mm(other, wu).astype(BF16)
    gate_ref[...] = mm(mine, wg)
    up_ref[...] = mm(mine, wu)


def forward_kernel(
    group_ref, target_ref, gate_ref, up_ref, recv_ref, own_ref, other_ref, hid_ref, out_ref, pick_ref, y_ref
):
    rows = hid_ref.shape[0]

    @pl.when(pl.program_id(0) == 0)
    def _():
        pick_ref[...] = ones_where(iota((2 * rows, 2 * rows), 0) == target_ref[...])
        gate = gate_ref[...] + recv_ref[0].astype(F32)
        up = up_ref[...] + recv_ref[1].astype(F32)
        hid_ref[...] = (gate * jax.nn.sigmoid(gate) * up).astype(BF16)

    group = group_ref[0]
    hidden = hid_ref[...]
    y_ref[pl.ds(pl.multiple_of(group * rows, 16), rows), :] = mm(hidden, own_ref[...], NT).astype(BF16)
    y_ref[pl.ds(pl.multiple_of((1 - group) * rows, 16), rows), :] = mm(hidden, other_ref[...], NT).astype(BF16)
    out_ref[...] = mm(pick_ref[...], y_ref[...]).astype(BF16)


def backward_kernel(
    group_ref, target_ref, grad_ref, gate_ref, up_ref, recv_ref, own_ref, other_ref, out_ref, dy_ref
):
    rows = gate_ref.shape[0]

    @pl.when(pl.program_id(0) == 0)
    def _():
        pick = ones_where(iota((2 * rows, 2 * rows), 1) == target_ref[...])
        dy_ref[...] = mm(pick, grad_ref[...]).astype(BF16)

    group = group_ref[0]
    mine = dy_ref[pl.ds(pl.multiple_of(group * rows, 16), rows), :]
    other = dy_ref[pl.ds(pl.multiple_of((1 - group) * rows, 16), rows), :]
    d_hidden = mm(mine, own_ref[...]) + mm(other, other_ref[...])
    gate = gate_ref[...] + recv_ref[0].astype(F32)
    up = up_ref[...] + recv_ref[1].astype(F32)
    sigma = jax.nn.sigmoid(gate)
    out_ref[0] = (d_hidden * up * sigma * (1.0 + gate * (1.0 - sigma))).astype(BF16)
    out_ref[1] = (d_hidden * (gate * sigma)).astype(BF16)


def down_kernel(group_ref, dy_mine_ref, dy_other_ref, hid_ref, mine_ref, send_ref):
    hidden = hid_ref[...]
    send_ref[...] = mm(dy_other_ref[...], hidden, TN).astype(BF16)
    mine_ref[...] = mm(dy_mine_ref[...], hidden, TN)


def input_grad_kernel(group_ref, target_ref, own_ref, recv_ref, wg_ref, wu_ref, out_ref):
    rows = own_ref.shape[1]
    width = out_ref.shape[2]
    mine = pl.program_id(0) == group_ref[0]
    d_gate = jnp.where(mine, own_ref[0], recv_ref[0])
    d_up = jnp.where(mine, own_ref[1], recv_ref[1])
    halves = []
    for h in range(2):
        lo = h * width
        halves.append(
            (mm(d_gate, wg_ref[lo : lo + width, :], NT) + mm(d_up, wu_ref[lo : lo + width, :], NT)).astype(BF16)
        )
    pick = ones_where(iota((2 * rows, 2 * rows), 0) == target_ref[...])
    out_ref[0] = mm(pick, jnp.concatenate(halves, axis=0)).astype(BF16)


def combine_out_kernel(peers, cap, slots_ref, gates_ref, back_ref, out_ref):
    places = places_in_rows(slots_ref[...], peers, cap)
    count = slots_ref.shape[0]
    rows, half = back_ref.shape
    at = iota((count, rows), 1)
    gates = gates_ref[...]
    for h in range(2):
        total = None
        for k, place in enumerate(places):
            term = gates[:, k : k + 1] * mm(ones_where(at == place + h * cap), back_ref[...])
            total = term if total is None else total + term
        out_ref[:, h * half : (h + 1) * half] = total.astype(BF16)


def combine_grad_kernel(peers, cap, slots_ref, back_ref, out_ref):
    places = places_in_rows(slots_ref[...], peers, cap)
    count = slots_ref.shape[0]
    _, rows, width = back_ref.shape
    at = iota((count, rows), 1)
    for h in range(2):
        pick = sum(jnp.where(at == place + h * cap, 1.0, 0.0) for place in places).astype(BF16)
        for part in range(2):
            lo = (2 * part + h) * width
            out_ref[:, lo : lo + width] = mm(pick, back_ref[part]).astype(BF16)


def split_width(tokens, out_grad, route_gates, route_slot, gate_weight, up_weight, down_weight):
    count, width = tokens.shape
    top = route_slot.shape[1]
    peers = lax.axis_size("expert")
    cap = capacity_of(count, top, peers)
    w_gate, w_up, w_down = gate_weight[0], up_weight[0], down_weight[0]
    half, hidden_width = w_gate.shape
    quarter = half // 2
    rows = peers * cap
    swap = [(0, 1), (1, 0)]
    group = lax.axis_index("dp").astype(I32).reshape(1)
    slots_t = route_slot.T
    place = jnp.arange(rows, dtype=I32)
    left = place + cap * (place // cap)
    target = jnp.concatenate([left, left + cap])
    target_col, target_row = target[:, None], target[None, :]
    tile = min(256, hidden_width)

    def shape(*dims, dtype=BF16):
        return jax.ShapeDtypeStruct(dims, dtype)

    one_step = (1,)
    tok_send = call(
        functools.partial(send_tokens_kernel, peers, cap),
        shape(2, 2 * rows, quarter),
        one_step,
        [whole(slots_t.shape), whole(tokens.shape)],
        whole((2, 2 * rows, quarter)),
        flops=2 * 2 * rows * 2 * count * half,
        moved=2 * (tokens.size + 2 * rows * half),
    )(slots_t, tokens)
    tok_recv = lax.all_to_all(
        tok_send.reshape(2 * peers, 2 * cap, quarter), ("dp", "expert"), 0, 0, tiled=True
    ).reshape(2, 2 * rows, quarter)
    down_other = lax.ppermute(w_down, "dp", swap)
    dy_send = call(
        functools.partial(send_grads_kernel, peers, cap),
        shape(2 * rows, half),
        one_step,
        [whole(slots_t.shape), whole(route_gates.shape), whole(out_grad.shape)],
        whole((2 * rows, half)),
        flops=2 * 2 * rows * 2 * count * half * top,
        moved=2 * (out_grad.size + 2 * rows * half),
    )(slots_t, route_gates, out_grad)
    dy_recv = lax.all_to_all(
        dy_send.reshape(peers, 2 * cap, half), "expert", 0, 0, tiled=True
    ).reshape(2 * rows, half)

    tiles = hidden_width // tile
    part_block = pl.BlockSpec((rows, tile), lambda i: (0, i))
    pair_block = pl.BlockSpec((2, rows, tile), lambda i: (0, 0, i))
    weight_block = pl.BlockSpec((half, tile), lambda i: (0, i))
    gate_mine, up_mine, part_send = call(
        partial_kernel,
        (shape(rows, hidden_width, dtype=F32), shape(rows, hidden_width, dtype=F32), shape(2, rows, hidden_width)),
        (tiles,),
        [SCALAR, whole((2 * rows, 1)), whole((2, 2 * rows, quarter)), weight_block, weight_block],
        (part_block, part_block, pair_block),
        [pltpu.VMEM((2 * rows, half), BF16)],
        flops=2 * 2 * rows * half * hidden_width * 2,
        moved=4 * half * hidden_width + 4 * rows * half,
    )(group, target_col, tok_recv, w_gate, w_up)
    part_recv = lax.ppermute(part_send, "dp", swap)

    step = min(512, half)
    down_rows = pl.BlockSpec((step, hidden_width), lambda i: (i, 0))
    hidden, y_send = call(
        forward_kernel,
        (shape(rows, hidden_width), shape(2 * rows, half)),
        (half // step,),
        [
            SCALAR,
            whole((1, 2 * rows)),
            whole((rows, hidden_width)),
            whole((rows, hidden_width)),
            whole((2, rows, hidden_width)),
            down_rows,
            down_rows,
        ],
        (whole((rows, hidden_width)), pl.BlockSpec((2 * rows, step), lambda i: (0, i))),
        [pltpu.VMEM((2 * rows, 2 * rows), BF16), pltpu.VMEM((2 * rows, step), BF16)],
        flops=2 * 2 * rows * half * hidden_width,
        moved=4 * half * hidden_width + 4 * rows * half,
    )(group, target_row, gate_mine, up_mine, part_recv, w_down, down_other)
    y_back = lax.all_to_all(
        y_send.reshape(peers, 2 * cap, half), "expert", 0, 0, tiled=True
    ).reshape(2 * rows, half)

    d_pair, dy_rows = call(
        backward_kernel,
        (shape(2, rows, hidden_width), shape(2 * rows, half)),
        (tiles,),
        [
            SCALAR,
            whole((2 * rows, 1)),
            whole((2 * rows, half)),
            part_block,
            part_block,
            pair_block,
            weight_block,
            weight_block,
        ],
        (pair_block, whole((2 * rows, half))),
        flops=2 * 2 * rows * half * hidden_width,
        moved=4 * half * hidden_width + 4 * rows * half,
    )(group, target_col, dy_recv, gate_mine, up_mine, part_recv, w_down, down_other)
    d_recv = lax.ppermute(d_pair, "dp", swap)
    dx_send = call(
        input_grad_kernel,
        shape(2, 2 * rows, quarter),
        (2,),
        [
            SCALAR,
            whole((1, 2 * rows)),
            whole((2, rows, hidden_width)),
            whole((2, rows, hidden_width)),
            whole((half, hidden_width)),
            whole((half, hidden_width)),
        ],
        pl.BlockSpec((1, 2 * rows, quarter), lambda i: (i, 0, 0)),
        flops=2 * 2 * rows * half * hidden_width * 2,
        moved=4 * half * hidden_width + 4 * rows * half,
    )(group, target_row, d_pair, d_recv, w_gate, w_up)
    dx_back = lax.all_to_all(
        dx_send.reshape(2 * peers, 2 * cap, quarter), ("dp", "expert"), 0, 0, tiled=True
    ).reshape(2, 2 * rows, quarter)

    strip = min(256, half)
    dy_pair = dy_rows.reshape(2, rows, half)
    dy_mine = lax.dynamic_index_in_dim(dy_pair, group[0], 0, keepdims=False)
    dy_other = lax.dynamic_index_in_dim(dy_pair, 1 - group[0], 0, keepdims=False)
    strip_block = pl.BlockSpec((rows, strip), lambda i: (0, i))
    grad_block = pl.BlockSpec((strip, hidden_width), lambda i: (i, 0))
    down_mine, down_send = call(
        down_kernel,
        (shape(half, hidden_width, dtype=F32), shape(half, hidden_width)),
        (half // strip,),
        [SCALAR, strip_block, strip_block, whole((rows, hidden_width))],
        (grad_block, grad_block),
        flops=2 * 2 * rows * half * hidden_width,
        moved=6 * half * hidden_width + 4 * rows * half,
    )(group, dy_mine, dy_other, hidden)
    down_recv = lax.ppermute(down_send, "dp", swap)
    down_grad = (down_mine + down_recv.astype(F32)).astype(BF16)[None]

    moe_out = call(
        functools.partial(combine_out_kernel, peers, cap),
        shape(count, width),
        one_step,
        [whole(route_slot.shape), whole(route_gates.shape), whole((2 * rows, half))],
        whole((count, width)),
        flops=2 * 2 * rows * count * half * 2 * top,
        moved=2 * (count * width + 2 * rows * half),
    )(route_slot, route_gates, y_back)
    token_grad = call(
        functools.partial(combine_grad_kernel, peers, cap),
        shape(count, width),
        one_step,
        [whole(route_slot.shape), whole((2, 2 * rows, quarter))],
        whole((count, width)),
        flops=2 * 2 * rows * count * half * 2,
        moved=2 * (count * width + 2 * rows * half),
    )(route_slot, dx_back)
    return (moe_out, token_grad, down_grad)


def capacity_of(count, top, peers):
    return max(2, (5 * count * top + 4 * peers - 1) // (4 * peers))


def expert_forward(rows_in, w_gate, w_up, w_down):
    gate_proj = jnp.dot(rows_in, w_gate, preferred_element_type=jnp.float32)
    up_proj = jnp.dot(rows_in, w_up, preferred_element_type=jnp.float32)
    sigma_gate = jax.nn.sigmoid(gate_proj)
    activated = gate_proj * sigma_gate
    hidden = (activated * up_proj).astype(jnp.bfloat16)
    outputs = lax.dot_general(
        hidden, w_down, (((1,), (1,)), ((), ())), preferred_element_type=jnp.float32
    ).astype(jnp.bfloat16)
    return (outputs, gate_proj, up_proj, hidden)


def expert_backward(rows_grad, gate_proj, up_proj, w_gate, w_up, w_down):
    grad_hidden = jnp.dot(rows_grad, w_down, preferred_element_type=jnp.float32)
    sigma_gate = jax.nn.sigmoid(gate_proj)
    activated = gate_proj * sigma_gate
    grad_gate = (
        grad_hidden * up_proj * sigma_gate * (1.0 + gate_proj * (1.0 - sigma_gate))
    ).astype(jnp.bfloat16)
    grad_up = (grad_hidden * activated).astype(jnp.bfloat16)
    contract_dims = (((1,), (1,)), ((), ()))
    summed = lax.dot_general(
        grad_gate, w_gate, contract_dims, preferred_element_type=jnp.float32
    ) + lax.dot_general(grad_up, w_up, contract_dims, preferred_element_type=jnp.float32)
    return summed.astype(jnp.bfloat16)


def gathered_weights(tokens, out_grad, route_gates, route_slot, gate_weight, up_weight, down_weight):
    tok_dev, model_width = tokens.shape
    route_count = route_slot.shape[1]
    peer_count = lax.axis_size("expert")
    capacity = capacity_of(tok_dev, route_count, peer_count)
    route_total = tok_dev * route_count
    send_rows = peer_count * capacity
    flat_slot = route_slot.reshape(-1)
    onehot = (flat_slot[:, None] == jnp.arange(peer_count, dtype=jnp.int32)[None, :]).astype(
        jnp.int32
    )
    slot_rank = jnp.sum((jnp.cumsum(onehot, axis=0) - onehot) * onehot, axis=1)
    send_index = flat_slot * capacity + slot_rank
    route_of_row = (
        jnp.full((send_rows,), route_total, jnp.int32)
        .at[send_index]
        .set(jnp.arange(route_total, dtype=jnp.int32))
    )
    filled = route_of_row < route_total
    safe_route = jnp.where(filled, route_of_row, 0)
    token_row = safe_route // route_count
    gate_value = jnp.where(filled, route_gates.reshape(-1)[safe_route], 0.0)
    rows_in = jnp.where(filled[:, None], tokens[token_row], jnp.zeros((), tokens.dtype))
    rows_in = rows_in.reshape(peer_count, capacity, model_width)
    rows_grad = (gate_value[:, None] * out_grad[token_row].astype(jnp.float32)).astype(jnp.bfloat16)
    rows_grad = rows_grad.reshape(peer_count, capacity, model_width)
    full_gate, full_up, full_down = (
        lax.all_gather(gate_weight, "dp", axis=1, tiled=True),
        lax.all_gather(up_weight, "dp", axis=1, tiled=True),
        lax.all_gather(down_weight, "dp", axis=1, tiled=True),
    )
    w_gate = full_gate[0]
    w_up = full_up[0]
    w_down = full_down[0]
    item_shape = (peer_count, capacity, model_width)
    received = lax.all_to_all(rows_in, "expert", split_axis=0, concat_axis=0, tiled=True)
    outputs, gate_proj, up_proj, hidden_saved = expert_forward(
        received.reshape(-1, model_width), w_gate, w_up, w_down
    )
    out_back = lax.all_to_all(
        outputs.reshape(item_shape), "expert", split_axis=0, concat_axis=0, tiled=True
    )
    grad_in = lax.all_to_all(rows_grad, "expert", split_axis=0, concat_axis=0, tiled=True)
    grad_rows = expert_backward(
        grad_in.reshape(-1, model_width), gate_proj, up_proj, w_gate, w_up, w_down
    )
    grad_back = lax.all_to_all(
        grad_rows.reshape(item_shape), "expert", split_axis=0, concat_axis=0, tiled=True
    )
    grad_flat = grad_in.reshape(-1, model_width)
    down_share = lax.psum_scatter(
        lax.dot_general(
            grad_flat, hidden_saved, (((0,), (0,)), ((), ())), preferred_element_type=jnp.float32
        ).astype(jnp.bfloat16),
        "dp",
        scatter_dimension=0,
        tiled=True,
    )
    down_grad = down_share[None]
    out_routes = out_back.reshape(send_rows, model_width)[send_index].astype(jnp.float32)
    out_routes = out_routes.reshape(tok_dev, route_count, model_width)
    moe_out = jnp.sum(route_gates[:, :, None] * out_routes, axis=1).astype(jnp.bfloat16)
    grad_routes = grad_back.reshape(send_rows, model_width)[send_index].astype(jnp.float32)
    token_grad = jnp.sum(grad_routes.reshape(tok_dev, route_count, model_width), axis=1).astype(
        jnp.bfloat16
    )
    return (moe_out, token_grad, down_grad)


def per_device(tokens, out_grad, route_gates, route_slot, gate_weight, up_weight, down_weight):
    count, _ = tokens.shape
    peers = lax.axis_size("expert")
    cap = capacity_of(count, route_slot.shape[1], peers)
    half, hidden_width = gate_weight.shape[1:]
    fits = (
        lax.axis_size("dp") == 2
        and cap % 4 == 0
        and (peers * cap) % 16 == 0
        and count % 128 == 0
        and half % 512 == 0
        and hidden_width % 256 == 0
    )
    plan = split_width if fits else gathered_weights
    return plan(tokens, out_grad, route_gates, route_slot, gate_weight, up_weight, down_weight)


def solution(mesh):
    placed = (
        P(("dp", "expert"), None),
        P(("dp", "expert"), None),
        P(("dp", "expert"), None),
        P(("dp", "expert"), None),
        P("expert", "dp", None),
        P("expert", "dp", None),
        P("expert", "dp", None),
    )
    return jax.shard_map(
        per_device,
        mesh=mesh,
        in_specs=placed,
        out_specs=(P(("dp", "expert"), None), P(("dp", "expert"), None), P("expert", "dp", None)),
        check_vma=False,
    )
```

```python
import functools

import jax
import jax.numpy as jnp
from jax import lax
from jax.experimental import pallas as pl
from jax.experimental.pallas import tpu as pltpu
from jax.sharding import PartitionSpec as P

PLANE = 4
F32, BF16, I32 = jnp.float32, jnp.bfloat16, jnp.int32
NT = (((1,), (1,)), ((), ()))
TN = (((0,), (0,)), ((), ()))


def mm(a, b, dims=(((1,), (0,)), ((), ()))):
    return lax.dot_general(a, b, dims, preferred_element_type=F32)


def ones_where(mask):
    return jnp.where(mask, 1.0, 0.0).astype(BF16)


def iota(shape, dim):
    return lax.broadcasted_iota(I32, shape, dim)


def call(kernel, out_shape, grid, in_specs, out_specs, scratch=(), flops=0, moved=0, vmem_mib=24):
    return pl.pallas_call(
        kernel,
        out_shape=out_shape,
        grid=grid,
        in_specs=in_specs,
        out_specs=out_specs,
        scratch_shapes=list(scratch),
        cost_estimate=pl.CostEstimate(flops=flops, bytes_accessed=moved, transcendentals=0),
        compiler_params=pltpu.CompilerParams(vmem_limit_bytes=vmem_mib * 2**20),
    )


def whole(shape):
    return pl.BlockSpec(shape, lambda *_: (0,) * len(shape))


def column_half(group, half):
    return pl.ds(pl.multiple_of(group * half, 128), half)


SCALAR = pl.BlockSpec(memory_space=pltpu.SMEM)
HBM = pl.BlockSpec(memory_space=pltpu.HBM)


def ranks_in_lanes(slots, peers):
    top, count = slots.shape
    named = [jnp.where(iota((peers, count), 0) == slots[k : k + 1, :], 1.0, 0.0) for k in range(top)]
    earlier = ones_where(iota((count, count), 0) < iota((count, count), 1))
    before = mm(sum(named).astype(BF16), earlier)
    return [jnp.sum(before * each, axis=0, keepdims=True).astype(I32) for each in named]


def ranks_in_rows(slots, peers):
    count, top = slots.shape
    named = [jnp.where(iota((count, peers), 1) == slots[:, k : k + 1], 1.0, 0.0) for k in range(top)]
    earlier = ones_where(iota((count, count), 1) < iota((count, count), 0))
    before = mm(earlier, sum(named).astype(BF16))
    return [jnp.sum(before * each, axis=1, keepdims=True).astype(I32) for each in named]


def masks_of(number, expert):
    return (number ^ expert) & (PLANE - 1), (number ^ expert) // PLANE


def spread(values, refs, columns, block):
    each = refs[0].shape[0]
    for m, ref in enumerate(refs):
        for i in range(each):
            lo = (each * m + i) * block
            ref[i, :, columns] = values[lo : lo + block].astype(BF16)


def send_tokens_kernel(peers, cap, slots_ref, tok_ref, out_ref):
    _, rows, width = out_ref.shape
    slots = slots_ref[...]
    at = iota((rows, slots.shape[1]), 0)
    places = [slots[k : k + 1, :] * (2 * cap) + rank for k, rank in enumerate(ranks_in_lanes(slots, peers))]
    halves = [sum(jnp.where(at == place + h * cap, 1.0, 0.0) for place in places) for h in range(2)]
    pick = jnp.concatenate(halves, axis=1).astype(BF16)
    for part in range(2):
        lo = part * 2 * width
        both = jnp.concatenate([tok_ref[:, lo : lo + width], tok_ref[:, lo + width : lo + 2 * width]], axis=0)
        out_ref[part] = mm(pick, both).astype(BF16)


def send_grads_kernel(peers, cap, group_ref, expert_ref, slots_ref, gates_ref, grad_ref, *out_refs):
    slots, gates = slots_ref[...], gates_ref[...]
    group, expert = group_ref[0], expert_ref[0]
    rows, count = 2 * cap * peers, slots.shape[1]
    half = out_refs[0].shape[2]
    at = iota((rows, count), 0)
    halves = [grad_ref[:, column_half(g, half)].astype(F32) for g in (group, 1 - group)]
    total = None
    for k, rank in enumerate(ranks_in_lanes(slots, peers)):
        near, far = masks_of(slots[k : k + 1, :], expert)
        place = (near * (peers // PLANE) + far) * (2 * cap) + rank
        pick = jnp.concatenate([jnp.where(at == place + o * cap, 1.0, 0.0) for o in range(2)], axis=1).astype(BF16)
        both = jnp.concatenate([(gates[:, k : k + 1] * each).astype(BF16) for each in halves], axis=0)
        rows_k = mm(pick, both)
        total = rows_k if total is None else total + rows_k
    spread(total, out_refs, slice(None), 2 * cap)


def regroup_kernel(count, *refs):
    blocks, outs = refs[:count], refs[count:]
    for i, out_ref in enumerate(outs):
        for m, block_ref in enumerate(blocks):
            out_ref[m] = block_ref[i]


def partial_kernel(
    tile, group_ref, target_ref, recv_ref, wg_ref, wu_ref, gate_ref, up_ref, send_ref, x_ref, w_ref, sems
):
    rows, ff = gate_ref.shape
    width = recv_ref.shape[2]
    copies = {}
    for t in range(ff // tile):
        columns = pl.ds(t * tile, tile)
        for i, ref in enumerate((wg_ref, wu_ref)):
            copies[t, i] = pltpu.make_async_copy(ref.at[:, columns], w_ref.at[i, :, columns], sems.at[i, t])
            copies[t, i].start()
    pick = ones_where(iota((2 * rows, 2 * rows), 1) == target_ref[...])
    for o, g in enumerate((group_ref[0], 1 - group_ref[0])):
        for h in range(2):
            x_ref[o * rows : (o + 1) * rows, h * width : (h + 1) * width] = mm(
                pick[h * rows : (h + 1) * rows], recv_ref[g]
            ).astype(BF16)
    for t in range(ff // tile):
        columns = slice(t * tile, (t + 1) * tile)
        for i, mine_ref in enumerate((gate_ref, up_ref)):
            copies[t, i].wait()
            both = mm(x_ref[...], w_ref[i, :, columns])
            mine_ref[:, columns] = both[:rows]
            send_ref[i, :, columns] = both[rows:].astype(BF16)


def backward_kernel(target_ref, gate_ref, up_ref, recv_ref, own_ref, other_ref, *refs):
    *came_refs, hid_ref, out_ref, dy_mine_ref, dy_send_ref, came_ref = refs
    rows = gate_ref.shape[0]

    @pl.when(pl.program_id(0) == 0)
    def _():
        each = came_refs[0].shape[0]
        for m, ref in enumerate(came_refs):
            came_ref[m * each : (m + 1) * each, :] = ref[...]
        pick = ones_where(iota((2 * rows, 2 * rows), 1) == target_ref[...])
        dy = mm(pick, came_ref[...]).astype(BF16)
        dy_mine_ref[...] = dy[:rows]
        dy_send_ref[...] = dy[rows:]

    gate = gate_ref[...] + recv_ref[0].astype(F32)
    up = up_ref[...] + recv_ref[1].astype(F32)
    sigma = jax.nn.sigmoid(gate)
    active = gate * sigma
    hid_ref[...] = (active * up).astype(BF16)
    d_hidden = mm(dy_mine_ref[...], own_ref[...]) + mm(dy_send_ref[...], other_ref[...])
    out_ref[0] = (d_hidden * up * sigma * (1.0 + gate * (1.0 - sigma))).astype(BF16)
    out_ref[1] = (d_hidden * active).astype(BF16)


def forward_kernel(target_ref, hid_ref, own_ref, other_ref, *refs):
    *out_refs, pick_ref, y_ref = refs
    rows = hid_ref.shape[0]

    @pl.when(pl.program_id(0) == 0)
    def _():
        pick_ref[...] = ones_where(iota((2 * rows, 2 * rows), 0) == target_ref[...])

    hidden = hid_ref[...]
    y_ref[:rows, :] = mm(hidden, own_ref[...], NT).astype(BF16)
    y_ref[rows:, :] = mm(hidden, other_ref[...], NT).astype(BF16)
    spread(mm(pick_ref[...], y_ref[...]), out_refs, slice(None), out_refs[0].shape[1])


def input_grad_kernel(group_ref, target_ref, own_ref, recv_ref, wg_ref, wu_ref, out_ref, d_ref, dx_ref):
    rows = own_ref.shape[1]
    width = out_ref.shape[2]
    for i in range(2):
        d_ref[i, :rows, :] = own_ref[i]
        d_ref[i, rows:, :] = recv_ref[i]
    for h in range(2):
        part = slice(h * width, (h + 1) * width)
        dx = (mm(d_ref[0], wg_ref[part, :], NT) + mm(d_ref[1], wu_ref[part, :], NT)).astype(BF16)
        for o in range(2):
            dx_ref[o, h * rows : (h + 1) * rows, :] = dx[o * rows : (o + 1) * rows]
    pick = ones_where(iota((2 * rows, 2 * rows), 0) == target_ref[...])
    group = group_ref[0]
    out_ref[group] = mm(pick, dx_ref[0]).astype(BF16)
    out_ref[1 - group] = mm(pick, dx_ref[1]).astype(BF16)


def down_kernel(mine_ref, recv_ref, hid_ref, hid_recv_ref, out_ref):
    out_ref[...] = (mm(mine_ref[...], hid_ref[...], TN) + mm(recv_ref[...], hid_recv_ref[...], TN)).astype(BF16)


def combine_out_kernel(peers, cap, group_ref, expert_ref, slots_ref, gates_ref, *refs):
    *came_refs, out_ref, came_ref = refs
    slots, gates = slots_ref[...], gates_ref[...]
    group, expert = group_ref[0], expert_ref[0]
    rows, half = came_ref.shape
    each = rows // len(came_refs)
    for m, ref in enumerate(came_refs):
        came_ref[m * each : (m + 1) * each, :] = ref[...]
    at = iota((slots.shape[0], rows), 1)
    places = []
    for k, rank in enumerate(ranks_in_rows(slots, peers)):
        near, far = masks_of(slots[:, k : k + 1], expert)
        places.append((near * (peers // PLANE) + far) * (2 * cap) + rank)
    for o, g in enumerate((group, 1 - group)):
        total = None
        for k, place in enumerate(places):
            term = gates[:, k : k + 1] * mm(ones_where(at == place + o * cap), came_ref[...])
            total = term if total is None else total + term
        out_ref[:, column_half(g, half)] = total.astype(BF16)


def combine_grad_kernel(peers, cap, slots_ref, back_ref, out_ref):
    slots = slots_ref[...]
    places = [slots[:, k : k + 1] * (2 * cap) + rank for k, rank in enumerate(ranks_in_rows(slots, peers))]
    _, rows, width = back_ref.shape
    at = iota((slots.shape[0], rows), 1)
    for h in range(2):
        pick = sum(jnp.where(at == place + h * cap, 1.0, 0.0) for place in places).astype(BF16)
        for part in range(2):
            lo = (2 * part + h) * width
            out_ref[:, lo : lo + width] = mm(pick, back_ref[part]).astype(BF16)


def split_width(tokens, out_grad, route_gates, route_slot, gate_weight, up_weight, down_weight):
    count, width = tokens.shape
    top = route_slot.shape[1]
    peers = lax.axis_size("expert")
    planes = peers // PLANE
    cap = capacity_of(count, top, peers)
    w_gate, w_up, w_down = gate_weight[0], up_weight[0], down_weight[0]
    half, ff = w_gate.shape
    quarter = half // 2
    rows = peers * cap
    swap = [(0, 1), (1, 0)]
    index = lax.axis_index("dp").astype(I32)
    group, expert = index.reshape(1), lax.axis_index("expert").astype(I32).reshape(1)
    slots_t = route_slot.T
    place = jnp.arange(rows, dtype=I32)
    straight_left = (place // cap) * (2 * cap) + place % cap
    straight = jnp.concatenate([straight_left, straight_left + cap])
    near, far = masks_of(place // cap, expert)
    moved_left = (far * PLANE + near) * (2 * cap) + place % cap
    moved = jnp.concatenate([moved_left, moved_left + cap])
    tile, strip, narrow = min(256, ff), min(512, half), min(256, half)
    matmul_flops = 2 * 2 * rows * half * ff
    route_flops = 2 * 2 * rows * 2 * count * half
    route_bytes = 2 * (tokens.size + 2 * rows * half)
    weight_bytes = 2 * half * ff

    def shape(*dims, dtype=BF16):
        return jax.ShapeDtypeStruct(dims, dtype)

    near_block, far_block = (planes, 2 * cap, half), (PLANE, 2 * cap, half)

    def exchange(blocks, stride):
        return [blocks[0]] + [
            lax.ppermute(blocks[m], "expert", [(i, i ^ (m * stride)) for i in range(peers)])
            for m in range(1, len(blocks))
        ]

    def regroup(blocks):
        outs, *rest = blocks[0].shape
        return call(
            functools.partial(regroup_kernel, len(blocks)),
            tuple(pltpu.HBM((len(blocks), *rest), BF16) for _ in range(outs)),
            (1,),
            [whole(blocks[0].shape)] * len(blocks),
            tuple(whole((len(blocks), *rest)) for _ in range(outs)),
            moved=8 * rows * half,
        )(*blocks)

    down_other = lax.ppermute(w_down, "dp", swap)
    dy_near = call(
        functools.partial(send_grads_kernel, peers, cap),
        tuple(shape(*near_block) for _ in range(PLANE)),
        (1,),
        [SCALAR, SCALAR, whole(slots_t.shape), whole(route_gates.shape), whole(out_grad.shape)],
        tuple(whole(near_block) for _ in range(PLANE)),
        flops=top * route_flops,
        moved=route_bytes,
    )(group, expert, slots_t, route_gates, out_grad)
    dy_far = regroup(exchange(dy_near, 1))

    tok_send = call(
        functools.partial(send_tokens_kernel, peers, cap),
        shape(2, 2 * rows, quarter),
        (1,),
        [whole(slots_t.shape), whole(tokens.shape)],
        whole((2, 2 * rows, quarter)),
        flops=route_flops,
        moved=route_bytes,
    )(slots_t, tokens)
    tok_recv = lax.all_to_all(
        tok_send.reshape(2 * peers, 2 * cap, quarter), ("dp", "expert"), 0, 0, tiled=True
    ).reshape(2, 2 * rows, quarter)
    tok_recv, dy_far = lax.optimization_barrier((tok_recv, dy_far))

    part_block = pl.BlockSpec((rows, tile), lambda i: (0, i))
    pair_block = pl.BlockSpec((2, rows, tile), lambda i: (0, 0, i))
    weight_block = pl.BlockSpec((half, tile), lambda i: (0, i))
    gate_mine, up_mine, part_send = call(
        functools.partial(partial_kernel, tile),
        (shape(rows, ff, dtype=F32), shape(rows, ff, dtype=F32), shape(2, rows, ff)),
        (1,),
        [SCALAR, whole((2 * rows, 1)), whole((2, 2 * rows, quarter)), HBM, HBM],
        (whole((rows, ff)), whole((rows, ff)), whole((2, rows, ff))),
        [
            pltpu.VMEM((2 * rows, half), BF16),
            pltpu.VMEM((2, half, ff), BF16),
            pltpu.SemaphoreType.DMA((2, ff // tile)),
        ],
        flops=2 * matmul_flops,
        moved=2 * weight_bytes + 4 * rows * half,
    )(group, straight[:, None], tok_recv, w_gate, w_up)
    part_recv = lax.ppermute(part_send, "dp", swap)
    dy_came = exchange(dy_far, PLANE)

    hidden, d_pair, dy_mine, dy_other = call(
        backward_kernel,
        (shape(rows, ff), shape(2, rows, ff), shape(rows, half), shape(rows, half)),
        (ff // tile,),
        [whole((2 * rows, 1)), part_block, part_block, pair_block, weight_block, weight_block]
        + [whole((PLANE * 2 * cap, half))] * planes,
        (part_block, pair_block, whole((rows, half)), whole((rows, half))),
        [pltpu.VMEM((2 * rows, half), BF16)],
        flops=matmul_flops,
        moved=2 * weight_bytes + 4 * rows * half,
    )(
        moved[:, None], gate_mine, up_mine, part_recv, w_down, down_other,
        *(came.reshape(PLANE * 2 * cap, half) for came in dy_came)
    )
    down_rows = pl.BlockSpec((strip, ff), lambda i: (i, 0))
    y_far = call(
        forward_kernel,
        tuple(shape(*far_block) for _ in range(planes)),
        (half // strip,),
        [whole((1, 2 * rows)), whole((rows, ff)), down_rows, down_rows],
        tuple(pl.BlockSpec((PLANE, 2 * cap, strip), lambda i: (0, 0, i)) for _ in range(planes)),
        [pltpu.VMEM((2 * rows, 2 * rows), BF16), pltpu.VMEM((2 * rows, strip), BF16)],
        flops=matmul_flops,
        moved=2 * weight_bytes + 4 * rows * half,
    )(moved[None, :], hidden, w_down, down_other)
    hidden_recv = lax.ppermute(hidden, "dp", swap)
    d_recv = lax.ppermute(d_pair, "dp", swap)
    dy_cross = lax.ppermute(dy_other, "dp", swap)

    *_, d_recv = lax.optimization_barrier((*y_far, d_recv))
    y_far_came = exchange(y_far, PLANE)
    dx_send = call(
        input_grad_kernel,
        shape(2, 2 * rows, quarter),
        (1,),
        [
            SCALAR,
            whole((1, 2 * rows)),
            whole((2, rows, ff)),
            whole((2, rows, ff)),
            whole((half, ff)),
            whole((half, ff)),
        ],
        whole((2, 2 * rows, quarter)),
        [pltpu.VMEM((2, 2 * rows, ff), BF16), pltpu.VMEM((2, 2 * rows, quarter), BF16)],
        flops=2 * matmul_flops,
        moved=2 * weight_bytes + 4 * rows * half,
    )(group, straight[None, :], d_pair, d_recv, w_gate, w_up)
    dx_send, y_far_came, hidden_recv = lax.optimization_barrier((dx_send, y_far_came, hidden_recv))
    y_came = exchange(regroup(y_far_came), 1)
    dx_back = lax.all_to_all(
        dx_send.reshape(2 * peers, 2 * cap, quarter), ("dp", "expert"), 0, 0, tiled=True
    ).reshape(2, 2 * rows, quarter)

    strip_block = pl.BlockSpec((rows, narrow), lambda i: (0, i))
    down_grad = call(
        down_kernel,
        shape(half, ff),
        (half // narrow,),
        [strip_block, strip_block, whole((rows, ff)), whole((rows, ff))],
        pl.BlockSpec((narrow, ff), lambda i: (i, 0)),
        flops=matmul_flops,
        moved=weight_bytes + 4 * rows * half,
    )(dy_mine, dy_cross, hidden, hidden_recv)[None]
    moe_out = call(
        functools.partial(combine_out_kernel, peers, cap),
        shape(count, width),
        (1,),
        [SCALAR, SCALAR, whole(route_slot.shape), whole(route_gates.shape)]
        + [whole((planes * 2 * cap, half))] * PLANE,
        whole((count, width)),
        [pltpu.VMEM((2 * rows, half), BF16)],
        flops=top * route_flops,
        moved=route_bytes,
    )(group, expert, route_slot, route_gates, *(came.reshape(planes * 2 * cap, half) for came in y_came))
    dx_back, moe_out, down_grad = lax.optimization_barrier((dx_back, moe_out, down_grad))
    token_grad = call(
        functools.partial(combine_grad_kernel, peers, cap),
        shape(count, width),
        (1,),
        [whole(route_slot.shape), whole((2, 2 * rows, quarter))],
        whole((count, width)),
        flops=route_flops,
        moved=route_bytes,
    )(route_slot, dx_back)
    return (moe_out, token_grad, down_grad)


def capacity_of(count, top, peers):
    return max(2, (5 * count * top + 4 * peers - 1) // (4 * peers))


def expert_forward(rows_in, w_gate, w_up, w_down):
    gate_proj = jnp.dot(rows_in, w_gate, preferred_element_type=jnp.float32)
    up_proj = jnp.dot(rows_in, w_up, preferred_element_type=jnp.float32)
    sigma_gate = jax.nn.sigmoid(gate_proj)
    activated = gate_proj * sigma_gate
    hidden = (activated * up_proj).astype(jnp.bfloat16)
    outputs = lax.dot_general(
        hidden, w_down, (((1,), (1,)), ((), ())), preferred_element_type=jnp.float32
    ).astype(jnp.bfloat16)
    return (outputs, gate_proj, up_proj, hidden)


def expert_backward(rows_grad, gate_proj, up_proj, w_gate, w_up, w_down):
    grad_hidden = jnp.dot(rows_grad, w_down, preferred_element_type=jnp.float32)
    sigma_gate = jax.nn.sigmoid(gate_proj)
    activated = gate_proj * sigma_gate
    grad_gate = (
        grad_hidden * up_proj * sigma_gate * (1.0 + gate_proj * (1.0 - sigma_gate))
    ).astype(jnp.bfloat16)
    grad_up = (grad_hidden * activated).astype(jnp.bfloat16)
    contract_dims = (((1,), (1,)), ((), ()))
    summed = lax.dot_general(
        grad_gate, w_gate, contract_dims, preferred_element_type=jnp.float32
    ) + lax.dot_general(grad_up, w_up, contract_dims, preferred_element_type=jnp.float32)
    return summed.astype(jnp.bfloat16)


def gathered_weights(tokens, out_grad, route_gates, route_slot, gate_weight, up_weight, down_weight):
    tok_dev, model_width = tokens.shape
    route_count = route_slot.shape[1]
    peer_count = lax.axis_size("expert")
    capacity = capacity_of(tok_dev, route_count, peer_count)
    route_total = tok_dev * route_count
    send_rows = peer_count * capacity
    flat_slot = route_slot.reshape(-1)
    onehot = (flat_slot[:, None] == jnp.arange(peer_count, dtype=jnp.int32)[None, :]).astype(
        jnp.int32
    )
    slot_rank = jnp.sum((jnp.cumsum(onehot, axis=0) - onehot) * onehot, axis=1)
    send_index = flat_slot * capacity + slot_rank
    route_of_row = (
        jnp.full((send_rows,), route_total, jnp.int32)
        .at[send_index]
        .set(jnp.arange(route_total, dtype=jnp.int32))
    )
    filled = route_of_row < route_total
    safe_route = jnp.where(filled, route_of_row, 0)
    token_row = safe_route // route_count
    gate_value = jnp.where(filled, route_gates.reshape(-1)[safe_route], 0.0)
    rows_in = jnp.where(filled[:, None], tokens[token_row], jnp.zeros((), tokens.dtype))
    rows_in = rows_in.reshape(peer_count, capacity, model_width)
    rows_grad = (gate_value[:, None] * out_grad[token_row].astype(jnp.float32)).astype(jnp.bfloat16)
    rows_grad = rows_grad.reshape(peer_count, capacity, model_width)
    full_gate, full_up, full_down = (
        lax.all_gather(gate_weight, "dp", axis=1, tiled=True),
        lax.all_gather(up_weight, "dp", axis=1, tiled=True),
        lax.all_gather(down_weight, "dp", axis=1, tiled=True),
    )
    w_gate = full_gate[0]
    w_up = full_up[0]
    w_down = full_down[0]
    item_shape = (peer_count, capacity, model_width)
    received = lax.all_to_all(rows_in, "expert", split_axis=0, concat_axis=0, tiled=True)
    outputs, gate_proj, up_proj, hidden_saved = expert_forward(
        received.reshape(-1, model_width), w_gate, w_up, w_down
    )
    out_back = lax.all_to_all(
        outputs.reshape(item_shape), "expert", split_axis=0, concat_axis=0, tiled=True
    )
    grad_in = lax.all_to_all(rows_grad, "expert", split_axis=0, concat_axis=0, tiled=True)
    grad_rows = expert_backward(
        grad_in.reshape(-1, model_width), gate_proj, up_proj, w_gate, w_up, w_down
    )
    grad_back = lax.all_to_all(
        grad_rows.reshape(item_shape), "expert", split_axis=0, concat_axis=0, tiled=True
    )
    grad_flat = grad_in.reshape(-1, model_width)
    down_share = lax.psum_scatter(
        lax.dot_general(
            grad_flat, hidden_saved, (((0,), (0,)), ((), ())), preferred_element_type=jnp.float32
        ).astype(jnp.bfloat16),
        "dp",
        scatter_dimension=0,
        tiled=True,
    )
    down_grad = down_share[None]
    out_routes = out_back.reshape(send_rows, model_width)[send_index].astype(jnp.float32)
    out_routes = out_routes.reshape(tok_dev, route_count, model_width)
    moe_out = jnp.sum(route_gates[:, :, None] * out_routes, axis=1).astype(jnp.bfloat16)
    grad_routes = grad_back.reshape(send_rows, model_width)[send_index].astype(jnp.float32)
    token_grad = jnp.sum(grad_routes.reshape(tok_dev, route_count, model_width), axis=1).astype(
        jnp.bfloat16
    )
    return (moe_out, token_grad, down_grad)


def per_device(tokens, out_grad, route_gates, route_slot, gate_weight, up_weight, down_weight):
    count, _ = tokens.shape
    peers = lax.axis_size("expert")
    cap = capacity_of(count, route_slot.shape[1], peers)
    half, hidden_width = gate_weight.shape[1:]
    fits = (
        lax.axis_size("dp") == 2
        and peers % PLANE == 0
        and peers & (peers - 1) == 0
        and cap % 4 == 0
        and (peers * cap) % 16 == 0
        and count % 128 == 0
        and half % 512 == 0
        and hidden_width % 256 == 0
    )
    plan = split_width if fits else gathered_weights
    return plan(tokens, out_grad, route_gates, route_slot, gate_weight, up_weight, down_weight)


def solution(mesh):
    placed = (
        P(("dp", "expert"), None),
        P(("dp", "expert"), None),
        P(("dp", "expert"), None),
        P(("dp", "expert"), None),
        P("expert", "dp", None),
        P("expert", "dp", None),
        P("expert", "dp", None),
    )
    return jax.shard_map(
        per_device,
        mesh=mesh,
        in_specs=placed,
        out_specs=(P(("dp", "expert"), None), P(("dp", "expert"), None), P("expert", "dp", None)),
        check_vma=False,
    )
```

```python
import functools

import jax
import jax.numpy as jnp
from jax import lax
from jax.experimental import pallas as pl
from jax.experimental.pallas import tpu as pltpu
from jax.sharding import PartitionSpec as P

PLANE = 4
F32, BF16, I32 = jnp.float32, jnp.bfloat16, jnp.int32
NT = (((1,), (1,)), ((), ()))
TN = (((0,), (0,)), ((), ()))


def mm(a, b, dims=(((1,), (0,)), ((), ()))):
    return lax.dot_general(a, b, dims, preferred_element_type=F32)


def ones_where(mask):
    return jnp.where(mask, 1.0, 0.0).astype(BF16)


def iota(shape, dim):
    return lax.broadcasted_iota(I32, shape, dim)


def call(kernel, out_shape, grid, in_specs, out_specs, scratch=(), flops=0, moved=0, vmem_mib=24):
    return pl.pallas_call(
        kernel,
        out_shape=out_shape,
        grid=grid,
        in_specs=in_specs,
        out_specs=out_specs,
        scratch_shapes=list(scratch),
        cost_estimate=pl.CostEstimate(flops=flops, bytes_accessed=moved, transcendentals=0),
        compiler_params=pltpu.CompilerParams(vmem_limit_bytes=vmem_mib * 2**20),
    )


def whole(shape):
    return pl.BlockSpec(shape, lambda *_: (0,) * len(shape))


def column_half(group, half):
    return pl.ds(pl.multiple_of(group * half, 128), half)


AHEAD_OF_PARTIAL, AHEAD_OF_BACKWARD, AHEAD_OF_REGROUP = (int(each) for each in (20e9, 8e9, 20e9))
SCALAR = pl.BlockSpec(memory_space=pltpu.SMEM)
HBM = pl.BlockSpec(memory_space=pltpu.HBM)


def ranks_in_lanes(slots, peers):
    top, count = slots.shape
    named = [jnp.where(iota((peers, count), 0) == slots[k : k + 1, :], 1.0, 0.0) for k in range(top)]
    earlier = ones_where(iota((count, count), 0) < iota((count, count), 1))
    before = mm(sum(named).astype(BF16), earlier)
    return [jnp.sum(before * each, axis=0, keepdims=True).astype(I32) for each in named]


def ranks_in_rows(slots, peers):
    count, top = slots.shape
    named = [jnp.where(iota((count, peers), 1) == slots[:, k : k + 1], 1.0, 0.0) for k in range(top)]
    earlier = ones_where(iota((count, count), 1) < iota((count, count), 0))
    before = mm(earlier, sum(named).astype(BF16))
    return [jnp.sum(before * each, axis=1, keepdims=True).astype(I32) for each in named]


def masks_of(number, expert):
    return (number ^ expert) & (PLANE - 1), (number ^ expert) // PLANE


def spread(values, refs, columns, block):
    each = refs[0].shape[0]
    for m, ref in enumerate(refs):
        for i in range(each):
            lo = (each * m + i) * block
            ref[i, :, columns] = values[lo : lo + block].astype(BF16)


def send_tokens_kernel(peers, cap, slots_ref, tok_ref, out_ref):
    _, rows, width = out_ref.shape
    slots = slots_ref[...]
    at = iota((rows, slots.shape[1]), 0)
    places = [slots[k : k + 1, :] * (2 * cap) + rank for k, rank in enumerate(ranks_in_lanes(slots, peers))]
    halves = [sum(jnp.where(at == place + h * cap, 1.0, 0.0) for place in places) for h in range(2)]
    pick = jnp.concatenate(halves, axis=1).astype(BF16)
    for part in range(2):
        lo = part * 2 * width
        both = jnp.concatenate([tok_ref[:, lo : lo + width], tok_ref[:, lo + width : lo + 2 * width]], axis=0)
        out_ref[part] = mm(pick, both).astype(BF16)


def send_grads_kernel(peers, cap, group_ref, expert_ref, slots_ref, gates_ref, grad_ref, *out_refs):
    slots, gates = slots_ref[...], gates_ref[...]
    group, expert = group_ref[0], expert_ref[0]
    rows, count = 2 * cap * peers, slots.shape[1]
    half = out_refs[0].shape[2]
    at = iota((rows, count), 0)
    halves = [grad_ref[:, column_half(g, half)].astype(F32) for g in (group, 1 - group)]
    total = None
    for k, rank in enumerate(ranks_in_lanes(slots, peers)):
        near, far = masks_of(slots[k : k + 1, :], expert)
        place = (near * (peers // PLANE) + far) * (2 * cap) + rank
        pick = jnp.concatenate([jnp.where(at == place + o * cap, 1.0, 0.0) for o in range(2)], axis=1).astype(BF16)
        both = jnp.concatenate([(gates[:, k : k + 1] * each).astype(BF16) for each in halves], axis=0)
        rows_k = mm(pick, both)
        total = rows_k if total is None else total + rows_k
    spread(total, out_refs, slice(None), 2 * cap)


def regroup_kernel(count, *refs):
    blocks, outs = refs[:count], refs[count:]
    for i, out_ref in enumerate(outs):
        for m, block_ref in enumerate(blocks):
            out_ref[m] = block_ref[i]


def pick_kernel(target_ref, out_ref):
    out_ref[...] = ones_where(iota(out_ref.shape, 1) == target_ref[...])


def partial_kernel(tile, group_ref, pick_ref, recv_ref, wg_ref, wu_ref, out_ref, x_ref, w_ref, sems):
    _, rows, ff = out_ref.shape
    width = recv_ref.shape[2]
    copies = {}
    for t in range(ff // tile):
        columns = pl.ds(t * tile, tile)
        for i, ref in enumerate((wg_ref, wu_ref)):
            copies[t, i] = pltpu.make_async_copy(ref.at[:, columns], w_ref.at[i, :, columns], sems.at[i, t])
            copies[t, i].start()
    for h in range(2):
        x_ref[:, h * width : (h + 1) * width] = mm(pick_ref[h * rows : (h + 1) * rows, :], recv_ref[0]).astype(BF16)
    for t in range(ff // tile):
        columns = slice(t * tile, (t + 1) * tile)
        for i in range(2):
            copies[t, i].wait()
            out_ref[i, :, columns] = mm(x_ref[...], w_ref[i, :, columns]).astype(out_ref.dtype)


def hidden_grad_kernel(target_ref, own_ref, other_ref, *refs):
    *came_refs, out_ref, dy_mine_ref, dy_send_ref, came_ref = refs
    rows = out_ref.shape[0]

    @pl.when(pl.program_id(0) == 0)
    def _():
        each = came_refs[0].shape[0]
        for m, ref in enumerate(came_refs):
            came_ref[m * each : (m + 1) * each, :] = ref[...]
        pick = ones_where(iota((2 * rows, 2 * rows), 1) == target_ref[...])
        dy = mm(pick, came_ref[...]).astype(BF16)
        dy_mine_ref[...] = dy[:rows]
        dy_send_ref[...] = dy[rows:]

    out_ref[...] = mm(dy_mine_ref[...], own_ref[...]) + mm(dy_send_ref[...], other_ref[...])


def pointwise_kernel(mine_ref, recv_ref, d_hidden_ref, hid_ref, out_ref):
    gate = mine_ref[0] + recv_ref[0].astype(F32)
    up = mine_ref[1] + recv_ref[1].astype(F32)
    sigma = jax.nn.sigmoid(gate)
    active = gate * sigma
    d_hidden = d_hidden_ref[...]
    out_ref[0] = (d_hidden * up * sigma * (1.0 + gate * (1.0 - sigma))).astype(BF16)
    out_ref[1] = (d_hidden * active).astype(BF16)
    hid_ref[...] = (active * up).astype(BF16)


def forward_kernel(target_ref, hid_ref, own_ref, other_ref, *refs):
    *out_refs, pick_ref, y_ref = refs
    rows = hid_ref.shape[0]

    @pl.when(pl.program_id(0) == 0)
    def _():
        pick_ref[...] = ones_where(iota((2 * rows, 2 * rows), 0) == target_ref[...])

    hidden = hid_ref[...]
    y_ref[:rows, :] = mm(hidden, own_ref[...], NT).astype(BF16)
    y_ref[rows:, :] = mm(hidden, other_ref[...], NT).astype(BF16)
    spread(mm(pick_ref[...], y_ref[...]), out_refs, slice(None), out_refs[0].shape[1])


def input_grad_kernel(other, group_ref, target_ref, d_ref, wg_ref, wu_ref, *refs):
    *_, out_ref, dx_ref = refs
    rows = d_ref.shape[1]
    width = out_ref.shape[2]
    for h in range(2):
        part = slice(h * width, (h + 1) * width)
        dx = mm(d_ref[0], wg_ref[part, :], NT) + mm(d_ref[1], wu_ref[part, :], NT)
        dx_ref[h * rows : (h + 1) * rows, :] = dx.astype(BF16)
    pick = ones_where(iota((2 * rows, 2 * rows), 0) == target_ref[...])
    out_ref[0] = mm(pick, dx_ref[...]).astype(BF16)


def down_kernel(mine_ref, recv_ref, hid_ref, hid_recv_ref, out_ref):
    out_ref[...] = (mm(mine_ref[...], hid_ref[...], TN) + mm(recv_ref[...], hid_recv_ref[...], TN)).astype(BF16)


def combine_out_kernel(peers, cap, group_ref, expert_ref, slots_ref, gates_ref, *refs):
    *came_refs, out_ref, came_ref = refs
    slots, gates = slots_ref[...], gates_ref[...]
    group, expert = group_ref[0], expert_ref[0]
    rows, half = came_ref.shape
    each = rows // len(came_refs)
    for m, ref in enumerate(came_refs):
        came_ref[m * each : (m + 1) * each, :] = ref[...]
    at = iota((slots.shape[0], rows), 1)
    places = []
    for k, rank in enumerate(ranks_in_rows(slots, peers)):
        near, far = masks_of(slots[:, k : k + 1], expert)
        places.append((near * (peers // PLANE) + far) * (2 * cap) + rank)
    for o, g in enumerate((group, 1 - group)):
        total = None
        for k, place in enumerate(places):
            term = gates[:, k : k + 1] * mm(ones_where(at == place + o * cap), came_ref[...])
            total = term if total is None else total + term
        out_ref[:, column_half(g, half)] = total.astype(BF16)


def combine_grad_kernel(peers, cap, slots_ref, back_ref, out_ref):
    slots = slots_ref[...]
    places = [slots[:, k : k + 1] * (2 * cap) + rank for k, rank in enumerate(ranks_in_rows(slots, peers))]
    _, rows, width = back_ref.shape
    at = iota((slots.shape[0], rows), 1)
    for h in range(2):
        pick = sum(jnp.where(at == place + h * cap, 1.0, 0.0) for place in places).astype(BF16)
        for part in range(2):
            lo = (2 * part + h) * width
            out_ref[:, lo : lo + width] = mm(pick, back_ref[part]).astype(BF16)


def split_width(tokens, out_grad, route_gates, route_slot, gate_weight, up_weight, down_weight):
    count, width = tokens.shape
    top = route_slot.shape[1]
    peers = lax.axis_size("expert")
    planes = peers // PLANE
    cap = capacity_of(count, top, peers)
    w_gate, w_up, w_down = gate_weight[0], up_weight[0], down_weight[0]
    half, ff = w_gate.shape
    quarter = half // 2
    rows = peers * cap
    swap = [(0, 1), (1, 0)]
    index = lax.axis_index("dp").astype(I32)
    group, expert = index.reshape(1), lax.axis_index("expert").astype(I32).reshape(1)
    slots_t = route_slot.T
    place = jnp.arange(rows, dtype=I32)
    straight_left = (place // cap) * (2 * cap) + place % cap
    straight = jnp.concatenate([straight_left, straight_left + cap])
    near, far = masks_of(place // cap, expert)
    moved_left = (far * PLANE + near) * (2 * cap) + place % cap
    moved = jnp.concatenate([moved_left, moved_left + cap])
    tile, strip, narrow = min(256, ff), min(512, half), min(256, half)
    matmul_flops = 2 * 2 * rows * half * ff
    route_flops = 2 * 2 * rows * 2 * count * half
    route_bytes = 2 * (tokens.size + 2 * rows * half)
    weight_bytes = 2 * half * ff

    def shape(*dims, dtype=BF16):
        return jax.ShapeDtypeStruct(dims, dtype)

    near_block, far_block = (planes, 2 * cap, half), (PLANE, 2 * cap, half)

    def exchange(blocks, stride):
        return [blocks[0]] + [
            lax.ppermute(blocks[m], "expert", [(i, i ^ (m * stride)) for i in range(peers)])
            for m in range(1, len(blocks))
        ]

    def regroup(blocks, hold=0):
        outs, *rest = blocks[0].shape
        return call(
            functools.partial(regroup_kernel, len(blocks)),
            tuple(pltpu.HBM((len(blocks), *rest), BF16) for _ in range(outs)),
            (1,),
            [whole(blocks[0].shape)] * len(blocks),
            tuple(whole((len(blocks), *rest)) for _ in range(outs)),
            flops=hold,
            moved=8 * rows * half,
        )(*blocks)

    down_other = lax.ppermute(w_down, "dp", swap)
    dy_near = call(
        functools.partial(send_grads_kernel, peers, cap),
        tuple(shape(*near_block) for _ in range(PLANE)),
        (1,),
        [SCALAR, SCALAR, whole(slots_t.shape), whole(route_gates.shape), whole(out_grad.shape)],
        tuple(whole(near_block) for _ in range(PLANE)),
        flops=top * route_flops,
        moved=route_bytes,
    )(group, expert, slots_t, route_gates, out_grad)
    dy_far = regroup(exchange(dy_near, 1))

    tok_send = call(
        functools.partial(send_tokens_kernel, peers, cap),
        shape(2, 2 * rows, quarter),
        (1,),
        [whole(slots_t.shape), whole(tokens.shape)],
        whole((2, 2 * rows, quarter)),
        flops=route_flops,
        moved=route_bytes,
    )(slots_t, tokens)
    tok_recv = lax.all_to_all(
        tok_send.reshape(2 * peers, 2 * cap, quarter), ("dp", "expert"), 0, 0, tiled=True
    ).reshape(2, 2 * rows, quarter)

    part_block = pl.BlockSpec((rows, tile), lambda i: (0, i))
    pair_block = pl.BlockSpec((2, rows, tile), lambda i: (0, 0, i))
    weight_block = pl.BlockSpec((half, tile), lambda i: (0, i))
    target, *_ = lax.optimization_barrier((straight[:, None], down_other, *dy_far))
    pick = call(
        pick_kernel,
        shape(2 * rows, 2 * rows),
        (1,),
        [whole((2 * rows, 1))],
        whole((2 * rows, 2 * rows)),
        flops=AHEAD_OF_PARTIAL,
        moved=8 * rows * rows,
    )(target)

    def partial(other, dtype, received, hold=0):
        return pl.pallas_call(
            functools.partial(partial_kernel, tile),
            out_shape=shape(2, rows, ff, dtype=dtype),
            grid_spec=pltpu.PrefetchScalarGridSpec(
                num_scalar_prefetch=1,
                grid=(1,),
                in_specs=[
                    whole((2 * rows, 2 * rows)),
                    pl.BlockSpec((1, 2 * rows, quarter), lambda i, g: (other ^ g[0], 0, 0)),
                    HBM,
                    HBM,
                ],
                out_specs=whole((2, rows, ff)),
                scratch_shapes=[
                    pltpu.VMEM((rows, half), BF16),
                    pltpu.VMEM((2, half, ff), BF16),
                    pltpu.SemaphoreType.DMA((2, ff // tile)),
                ],
            ),
            cost_estimate=pl.CostEstimate(
                flops=matmul_flops + hold, bytes_accessed=2 * weight_bytes + 2 * rows * half, transcendentals=0
            ),
            compiler_params=pltpu.CompilerParams(vmem_limit_bytes=24 * 2**20),
        )(
            group,
            pick,
            received,
            pltpu.with_memory_space_constraint(w_gate, pltpu.HBM),
            pltpu.with_memory_space_constraint(w_up, pltpu.HBM),
        )

    part_send = partial(1, BF16, tok_recv)
    part_recv = lax.ppermute(part_send, "dp", swap)
    dy_came = exchange(dy_far, PLANE)
    part_mine = partial(0, F32, tok_recv)

    d_hidden, dy_mine, dy_other = call(
        hidden_grad_kernel,
        (shape(rows, ff, dtype=F32), shape(rows, half), shape(rows, half)),
        (ff // tile,),
        [whole((2 * rows, 1)), weight_block, weight_block] + [whole((PLANE * 2 * cap, half))] * planes,
        (part_block, whole((rows, half)), whole((rows, half))),
        [pltpu.VMEM((2 * rows, half), BF16)],
        flops=matmul_flops + AHEAD_OF_BACKWARD,
        moved=2 * weight_bytes + 4 * rows * half,
    )(moved[:, None], w_down, down_other, *(came.reshape(PLANE * 2 * cap, half) for came in dy_came))
    hidden, d_pair = call(
        pointwise_kernel,
        (shape(rows, ff), shape(2, rows, ff)),
        (ff // tile,),
        [pair_block, pair_block, part_block],
        (part_block, pair_block),
        flops=20 * rows * ff,
        moved=22 * rows * ff,
    )(part_mine, part_recv, d_hidden)
    down_rows = pl.BlockSpec((strip, ff), lambda i: (i, 0))
    y_far = call(
        forward_kernel,
        tuple(shape(*far_block) for _ in range(planes)),
        (half // strip,),
        [whole((1, 2 * rows)), whole((rows, ff)), down_rows, down_rows],
        tuple(pl.BlockSpec((PLANE, 2 * cap, strip), lambda i: (0, 0, i)) for _ in range(planes)),
        [pltpu.VMEM((2 * rows, 2 * rows), BF16), pltpu.VMEM((2 * rows, strip), BF16)],
        flops=matmul_flops,
        moved=2 * weight_bytes + 4 * rows * half,
    )(moved[None, :], hidden, w_down, down_other)
    hidden_recv = lax.ppermute(hidden, "dp", swap)
    d_recv = lax.ppermute(d_pair, "dp", swap)
    dy_other, _ = lax.optimization_barrier((dy_other, d_pair))
    dy_cross = lax.ppermute(dy_other, "dp", swap)

    *_, d_recv = lax.optimization_barrier((*y_far, d_recv))
    y_far_came = exchange(y_far, PLANE)
    def input_grad(other, d_rows, *before):
        return pl.pallas_call(
            functools.partial(input_grad_kernel, other),
            out_shape=shape(2, 2 * rows, quarter),
            grid_spec=pltpu.PrefetchScalarGridSpec(
                num_scalar_prefetch=1,
                grid=(1,),
                in_specs=[
                    whole((1, 2 * rows)),
                    whole((2, rows, ff)),
                    whole((half, ff)),
                    whole((half, ff)),
                    *[HBM for _ in before],
                ],
                out_specs=pl.BlockSpec((1, 2 * rows, quarter), lambda i, g: (other ^ g[0], 0, 0)),
                scratch_shapes=[pltpu.VMEM((2 * rows, quarter), BF16)],
            ),
            input_output_aliases={5: 0} if before else {},
            cost_estimate=pl.CostEstimate(
                flops=matmul_flops, bytes_accessed=2 * weight_bytes + 2 * rows * half, transcendentals=0
            ),
            compiler_params=pltpu.CompilerParams(vmem_limit_bytes=24 * 2**20),
        )(group, straight[None, :], d_rows, w_gate, w_up, *before)

    dx_send = input_grad(1, d_recv, input_grad(0, d_pair))
    y_far_done = y_far_came
    _, *y_far_came = lax.optimization_barrier((dy_cross, *y_far_came))
    y_near = regroup(y_far_came, AHEAD_OF_REGROUP)
    y_came = exchange(y_near, 1)
    dx_back = lax.all_to_all(
        dx_send.reshape(2 * peers, 2 * cap, quarter), ("dp", "expert"), 0, 0, tiled=True
    ).reshape(2, 2 * rows, quarter)

    strip_block = pl.BlockSpec((rows, narrow), lambda i: (0, i))
    down_grad = call(
        down_kernel,
        shape(half, ff),
        (half // narrow,),
        [strip_block, strip_block, whole((rows, ff)), whole((rows, ff))],
        pl.BlockSpec((narrow, ff), lambda i: (i, 0)),
        flops=matmul_flops,
        moved=weight_bytes + 4 * rows * half,
    )(dy_mine, dy_cross, hidden, hidden_recv)[None]
    moe_out = call(
        functools.partial(combine_out_kernel, peers, cap),
        shape(count, width),
        (1,),
        [SCALAR, SCALAR, whole(route_slot.shape), whole(route_gates.shape)]
        + [whole((planes * 2 * cap, half))] * PLANE,
        whole((count, width)),
        [pltpu.VMEM((2 * rows, half), BF16)],
        flops=top * route_flops,
        moved=route_bytes,
    )(group, expert, route_slot, route_gates, *(came.reshape(planes * 2 * cap, half) for came in y_came))
    token_grad = call(
        functools.partial(combine_grad_kernel, peers, cap),
        shape(count, width),
        (1,),
        [whole(route_slot.shape), whole((2, 2 * rows, quarter))],
        whole((count, width)),
        flops=route_flops,
        moved=route_bytes,
    )(route_slot, dx_back)
    return (moe_out, token_grad, down_grad)


def capacity_of(count, top, peers):
    return max(2, (5 * count * top + 4 * peers - 1) // (4 * peers))


def expert_forward(rows_in, w_gate, w_up, w_down):
    gate_proj = jnp.dot(rows_in, w_gate, preferred_element_type=jnp.float32)
    up_proj = jnp.dot(rows_in, w_up, preferred_element_type=jnp.float32)
    sigma_gate = jax.nn.sigmoid(gate_proj)
    activated = gate_proj * sigma_gate
    hidden = (activated * up_proj).astype(jnp.bfloat16)
    outputs = lax.dot_general(
        hidden, w_down, (((1,), (1,)), ((), ())), preferred_element_type=jnp.float32
    ).astype(jnp.bfloat16)
    return (outputs, gate_proj, up_proj, hidden)


def expert_backward(rows_grad, gate_proj, up_proj, w_gate, w_up, w_down):
    grad_hidden = jnp.dot(rows_grad, w_down, preferred_element_type=jnp.float32)
    sigma_gate = jax.nn.sigmoid(gate_proj)
    activated = gate_proj * sigma_gate
    grad_gate = (
        grad_hidden * up_proj * sigma_gate * (1.0 + gate_proj * (1.0 - sigma_gate))
    ).astype(jnp.bfloat16)
    grad_up = (grad_hidden * activated).astype(jnp.bfloat16)
    contract_dims = (((1,), (1,)), ((), ()))
    summed = lax.dot_general(
        grad_gate, w_gate, contract_dims, preferred_element_type=jnp.float32
    ) + lax.dot_general(grad_up, w_up, contract_dims, preferred_element_type=jnp.float32)
    return summed.astype(jnp.bfloat16)


def gathered_weights(tokens, out_grad, route_gates, route_slot, gate_weight, up_weight, down_weight):
    tok_dev, model_width = tokens.shape
    route_count = route_slot.shape[1]
    peer_count = lax.axis_size("expert")
    capacity = capacity_of(tok_dev, route_count, peer_count)
    route_total = tok_dev * route_count
    send_rows = peer_count * capacity
    flat_slot = route_slot.reshape(-1)
    onehot = (flat_slot[:, None] == jnp.arange(peer_count, dtype=jnp.int32)[None, :]).astype(
        jnp.int32
    )
    slot_rank = jnp.sum((jnp.cumsum(onehot, axis=0) - onehot) * onehot, axis=1)
    send_index = flat_slot * capacity + slot_rank
    route_of_row = (
        jnp.full((send_rows,), route_total, jnp.int32)
        .at[send_index]
        .set(jnp.arange(route_total, dtype=jnp.int32))
    )
    filled = route_of_row < route_total
    safe_route = jnp.where(filled, route_of_row, 0)
    token_row = safe_route // route_count
    gate_value = jnp.where(filled, route_gates.reshape(-1)[safe_route], 0.0)
    rows_in = jnp.where(filled[:, None], tokens[token_row], jnp.zeros((), tokens.dtype))
    rows_in = rows_in.reshape(peer_count, capacity, model_width)
    rows_grad = (gate_value[:, None] * out_grad[token_row].astype(jnp.float32)).astype(jnp.bfloat16)
    rows_grad = rows_grad.reshape(peer_count, capacity, model_width)
    full_gate, full_up, full_down = (
        lax.all_gather(gate_weight, "dp", axis=1, tiled=True),
        lax.all_gather(up_weight, "dp", axis=1, tiled=True),
        lax.all_gather(down_weight, "dp", axis=1, tiled=True),
    )
    w_gate = full_gate[0]
    w_up = full_up[0]
    w_down = full_down[0]
    item_shape = (peer_count, capacity, model_width)
    received = lax.all_to_all(rows_in, "expert", split_axis=0, concat_axis=0, tiled=True)
    outputs, gate_proj, up_proj, hidden_saved = expert_forward(
        received.reshape(-1, model_width), w_gate, w_up, w_down
    )
    out_back = lax.all_to_all(
        outputs.reshape(item_shape), "expert", split_axis=0, concat_axis=0, tiled=True
    )
    grad_in = lax.all_to_all(rows_grad, "expert", split_axis=0, concat_axis=0, tiled=True)
    grad_rows = expert_backward(
        grad_in.reshape(-1, model_width), gate_proj, up_proj, w_gate, w_up, w_down
    )
    grad_back = lax.all_to_all(
        grad_rows.reshape(item_shape), "expert", split_axis=0, concat_axis=0, tiled=True
    )
    grad_flat = grad_in.reshape(-1, model_width)
    down_share = lax.psum_scatter(
        lax.dot_general(
            grad_flat, hidden_saved, (((0,), (0,)), ((), ())), preferred_element_type=jnp.float32
        ).astype(jnp.bfloat16),
        "dp",
        scatter_dimension=0,
        tiled=True,
    )
    down_grad = down_share[None]
    out_routes = out_back.reshape(send_rows, model_width)[send_index].astype(jnp.float32)
    out_routes = out_routes.reshape(tok_dev, route_count, model_width)
    moe_out = jnp.sum(route_gates[:, :, None] * out_routes, axis=1).astype(jnp.bfloat16)
    grad_routes = grad_back.reshape(send_rows, model_width)[send_index].astype(jnp.float32)
    token_grad = jnp.sum(grad_routes.reshape(tok_dev, route_count, model_width), axis=1).astype(
        jnp.bfloat16
    )
    return (moe_out, token_grad, down_grad)


def per_device(tokens, out_grad, route_gates, route_slot, gate_weight, up_weight, down_weight):
    count, _ = tokens.shape
    peers = lax.axis_size("expert")
    cap = capacity_of(count, route_slot.shape[1], peers)
    half, hidden_width = gate_weight.shape[1:]
    fits = (
        lax.axis_size("dp") == 2
        and peers % PLANE == 0
        and peers & (peers - 1) == 0
        and cap % 4 == 0
        and (peers * cap) % 16 == 0
        and count % 128 == 0
        and half % 512 == 0
        and hidden_width % 256 == 0
    )
    plan = split_width if fits else gathered_weights
    return plan(tokens, out_grad, route_gates, route_slot, gate_weight, up_weight, down_weight)


def solution(mesh):
    placed = (
        P(("dp", "expert"), None),
        P(("dp", "expert"), None),
        P(("dp", "expert"), None),
        P(("dp", "expert"), None),
        P("expert", "dp", None),
        P("expert", "dp", None),
        P("expert", "dp", None),
    )
    return jax.shard_map(
        per_device,
        mesh=mesh,
        in_specs=placed,
        out_specs=(P(("dp", "expert"), None), P(("dp", "expert"), None), P("expert", "dp", None)),
        check_vma=False,
    )
```

```python
import functools

import jax
import jax.numpy as jnp
from jax import lax
from jax.experimental import pallas as pl
from jax.experimental.pallas import tpu as pltpu
from jax.sharding import PartitionSpec as P

PLANE = 4
F32, BF16, I32 = jnp.float32, jnp.bfloat16, jnp.int32
NT = (((1,), (1,)), ((), ()))
TN = (((0,), (0,)), ((), ()))


def mm(a, b, dims=(((1,), (0,)), ((), ()))):
    return lax.dot_general(a, b, dims, preferred_element_type=F32)


def ones_where(mask):
    return jnp.where(mask, 1.0, 0.0).astype(BF16)


def iota(shape, dim):
    return lax.broadcasted_iota(I32, shape, dim)


def call(kernel, out_shape, grid, in_specs, out_specs, scratch=(), flops=0, moved=0, vmem_mib=24):
    return pl.pallas_call(
        kernel,
        out_shape=out_shape,
        grid=grid,
        in_specs=in_specs,
        out_specs=out_specs,
        scratch_shapes=list(scratch),
        cost_estimate=pl.CostEstimate(flops=flops, bytes_accessed=moved, transcendentals=0),
        compiler_params=pltpu.CompilerParams(vmem_limit_bytes=vmem_mib * 2**20),
    )


def whole(shape):
    return pl.BlockSpec(shape, lambda *_: (0,) * len(shape))


def column_half(group, half):
    return pl.ds(pl.multiple_of(group * half, 128), half)


AHEAD_OF_PARTIAL, AHEAD_OF_BACKWARD, AHEAD_OF_REGROUP = (int(each) for each in (20e9, 8e9, 20e9))
SCALAR = pl.BlockSpec(memory_space=pltpu.SMEM)
HBM = pl.BlockSpec(memory_space=pltpu.HBM)


def ranks_in_lanes(slots, peers):
    top, count = slots.shape
    named = [jnp.where(iota((peers, count), 0) == slots[k : k + 1, :], 1.0, 0.0) for k in range(top)]
    earlier = ones_where(iota((count, count), 0) < iota((count, count), 1))
    before = mm(sum(named).astype(BF16), earlier)
    return [jnp.sum(before * each, axis=0, keepdims=True).astype(I32) for each in named]


def ranks_in_rows(slots, peers):
    count, top = slots.shape
    named = [jnp.where(iota((count, peers), 1) == slots[:, k : k + 1], 1.0, 0.0) for k in range(top)]
    earlier = ones_where(iota((count, count), 1) < iota((count, count), 0))
    before = mm(earlier, sum(named).astype(BF16))
    return [jnp.sum(before * each, axis=1, keepdims=True).astype(I32) for each in named]


def masks_of(number, expert):
    return (number ^ expert) & (PLANE - 1), (number ^ expert) // PLANE


def spread(values, refs, columns, block):
    each = refs[0].shape[0]
    for m, ref in enumerate(refs):
        for i in range(each):
            lo = (each * m + i) * block
            ref[i, :, columns] = values[lo : lo + block].astype(BF16)


def send_tokens_kernel(peers, cap, slots_ref, tok_ref, out_ref):
    _, rows, width = out_ref.shape
    slots = slots_ref[...]
    at = iota((rows, slots.shape[1]), 0)
    places = [slots[k : k + 1, :] * (2 * cap) + rank for k, rank in enumerate(ranks_in_lanes(slots, peers))]
    halves = [sum(jnp.where(at == place + h * cap, 1.0, 0.0) for place in places) for h in range(2)]
    pick = jnp.concatenate(halves, axis=1).astype(BF16)
    for part in range(2):
        lo = part * 2 * width
        both = jnp.concatenate([tok_ref[:, lo : lo + width], tok_ref[:, lo + width : lo + 2 * width]], axis=0)
        out_ref[part] = mm(pick, both).astype(BF16)


def send_grads_kernel(peers, cap, group_ref, expert_ref, slots_ref, gates_ref, grad_ref, *out_refs):
    slots, gates = slots_ref[...], gates_ref[...]
    group, expert = group_ref[0], expert_ref[0]
    rows, count = 2 * cap * peers, slots.shape[1]
    half = out_refs[0].shape[2]
    at = iota((rows, count), 0)
    halves = [grad_ref[:, column_half(g, half)].astype(F32) for g in (group, 1 - group)]
    total = None
    for k, rank in enumerate(ranks_in_lanes(slots, peers)):
        near, far = masks_of(slots[k : k + 1, :], expert)
        place = (near * (peers // PLANE) + far) * (2 * cap) + rank
        pick = jnp.concatenate([jnp.where(at == place + o * cap, 1.0, 0.0) for o in range(2)], axis=1).astype(BF16)
        both = jnp.concatenate([(gates[:, k : k + 1] * each).astype(BF16) for each in halves], axis=0)
        rows_k = mm(pick, both)
        total = rows_k if total is None else total + rows_k
    spread(total, out_refs, slice(None), 2 * cap)


def regroup_kernel(count, *refs):
    blocks, outs = refs[:count], refs[count:]
    for i, out_ref in enumerate(outs):
        for m, block_ref in enumerate(blocks):
            out_ref[m] = block_ref[i]


def pick_kernel(target_ref, out_ref):
    out_ref[...] = ones_where(iota(out_ref.shape, 1) == target_ref[...])


def partial_kernel(tile, group_ref, pick_ref, recv_ref, wg_ref, wu_ref, out_ref, x_ref, w_ref, sems):
    _, rows, ff = out_ref.shape
    width = recv_ref.shape[2]
    copies = {}
    for t in range(ff // tile):
        columns = pl.ds(t * tile, tile)
        for i, ref in enumerate((wg_ref, wu_ref)):
            copies[t, i] = pltpu.make_async_copy(ref.at[:, columns], w_ref.at[i, :, columns], sems.at[i, t])
            copies[t, i].start()
    for h in range(2):
        x_ref[:, h * width : (h + 1) * width] = mm(pick_ref[h * rows : (h + 1) * rows, :], recv_ref[0]).astype(BF16)
    for t in range(ff // tile):
        columns = slice(t * tile, (t + 1) * tile)
        for i in range(2):
            copies[t, i].wait()
            out_ref[i, :, columns] = mm(x_ref[...], w_ref[i, :, columns]).astype(out_ref.dtype)


def hidden_grad_kernel(target_ref, own_ref, other_0_ref, other_1_ref, *refs):
    *came_refs, out_ref, dy_mine_ref, dy_send_ref, came_ref = refs
    rows = out_ref.shape[0]

    @pl.when(pl.program_id(0) == 0)
    def _():
        each = came_refs[0].shape[0]
        for m, ref in enumerate(came_refs):
            came_ref[m * each : (m + 1) * each, :] = ref[...]
        pick = ones_where(iota((2 * rows, 2 * rows), 1) == target_ref[...])
        dy = mm(pick, came_ref[...]).astype(BF16)
        dy_mine_ref[...] = dy[:rows]
        dy_send_ref[...] = dy[rows:]

    cut = other_0_ref.shape[0]
    total = mm(dy_mine_ref[...], own_ref[...])
    total = total + mm(dy_send_ref[:, :cut], other_0_ref[...])
    out_ref[...] = total + mm(dy_send_ref[:, cut:], other_1_ref[...])


def pointwise_kernel(mine_ref, recv_ref, d_hidden_ref, hid_ref, out_ref):
    gate = mine_ref[0] + recv_ref[0].astype(F32)
    up = mine_ref[1] + recv_ref[1].astype(F32)
    sigma = jax.nn.sigmoid(gate)
    active = gate * sigma
    d_hidden = d_hidden_ref[...]
    out_ref[0] = (d_hidden * up * sigma * (1.0 + gate * (1.0 - sigma))).astype(BF16)
    out_ref[1] = (d_hidden * active).astype(BF16)
    hid_ref[...] = (active * up).astype(BF16)


def forward_kernel(target_ref, hid_ref, own_ref, other_0_ref, other_1_ref, *refs):
    *out_refs, y_ref = refs
    rows = hid_ref.shape[0]
    cut = other_0_ref.shape[0]
    pick = ones_where(iota((2 * rows, 2 * rows), 0) == target_ref[...])
    for i, other_ref in enumerate((other_0_ref, other_1_ref)):
        columns = slice(i * cut, (i + 1) * cut)
        y_ref[:rows, :] = mm(hid_ref[...], own_ref[columns, :], NT).astype(BF16)
        y_ref[rows:, :] = mm(hid_ref[...], other_ref[...], NT).astype(BF16)
        spread(mm(pick, y_ref[...]), out_refs, columns, out_refs[0].shape[1])


def input_grad_kernel(other, group_ref, target_ref, d_ref, wg_ref, wu_ref, *refs):
    *_, out_ref, dx_ref = refs
    rows = d_ref.shape[1]
    width = out_ref.shape[2]
    for h in range(2):
        part = slice(h * width, (h + 1) * width)
        dx = mm(d_ref[0], wg_ref[part, :], NT) + mm(d_ref[1], wu_ref[part, :], NT)
        dx_ref[h * rows : (h + 1) * rows, :] = dx.astype(BF16)
    pick = ones_where(iota((2 * rows, 2 * rows), 0) == target_ref[...])
    out_ref[0] = mm(pick, dx_ref[...]).astype(BF16)


def down_kernel(mine_ref, recv_ref, hid_ref, hid_recv_ref, out_ref):
    out_ref[...] = (mm(mine_ref[...], hid_ref[...], TN) + mm(recv_ref[...], hid_recv_ref[...], TN)).astype(BF16)


def combine_out_kernel(peers, cap, group_ref, expert_ref, slots_ref, gates_ref, *refs):
    *came_refs, out_ref, came_ref = refs
    slots, gates = slots_ref[...], gates_ref[...]
    group, expert = group_ref[0], expert_ref[0]
    rows, half = came_ref.shape
    each = rows // len(came_refs)
    for m, ref in enumerate(came_refs):
        came_ref[m * each : (m + 1) * each, :] = ref[...]
    at = iota((slots.shape[0], rows), 1)
    places = []
    for k, rank in enumerate(ranks_in_rows(slots, peers)):
        near, far = masks_of(slots[:, k : k + 1], expert)
        places.append((near * (peers // PLANE) + far) * (2 * cap) + rank)
    for o, g in enumerate((group, 1 - group)):
        total = None
        for k, place in enumerate(places):
            term = gates[:, k : k + 1] * mm(ones_where(at == place + o * cap), came_ref[...])
            total = term if total is None else total + term
        out_ref[:, column_half(g, half)] = total.astype(BF16)


def combine_grad_kernel(peers, cap, slots_ref, back_ref, out_ref):
    slots = slots_ref[...]
    places = [slots[:, k : k + 1] * (2 * cap) + rank for k, rank in enumerate(ranks_in_rows(slots, peers))]
    _, rows, width = back_ref.shape
    at = iota((slots.shape[0], rows), 1)
    for h in range(2):
        pick = sum(jnp.where(at == place + h * cap, 1.0, 0.0) for place in places).astype(BF16)
        for part in range(2):
            lo = (2 * part + h) * width
            out_ref[:, lo : lo + width] = mm(pick, back_ref[part]).astype(BF16)


def split_width(tokens, out_grad, route_gates, route_slot, gate_weight, up_weight, down_weight):
    count, width = tokens.shape
    top = route_slot.shape[1]
    peers = lax.axis_size("expert")
    planes = peers // PLANE
    cap = capacity_of(count, top, peers)
    w_gate, w_up, w_down = gate_weight[0], up_weight[0], down_weight[0]
    half, ff = w_gate.shape
    quarter = half // 2
    rows = peers * cap
    swap = [(0, 1), (1, 0)]
    index = lax.axis_index("dp").astype(I32)
    group, expert = index.reshape(1), lax.axis_index("expert").astype(I32).reshape(1)
    slots_t = route_slot.T
    place = jnp.arange(rows, dtype=I32)
    straight_left = (place // cap) * (2 * cap) + place % cap
    straight = jnp.concatenate([straight_left, straight_left + cap])
    near, far = masks_of(place // cap, expert)
    moved_left = (far * PLANE + near) * (2 * cap) + place % cap
    moved = jnp.concatenate([moved_left, moved_left + cap])
    tile, narrow = min(256, ff), min(256, half)
    matmul_flops = 2 * 2 * rows * half * ff
    route_flops = 2 * 2 * rows * 2 * count * half
    route_bytes = 2 * (tokens.size + 2 * rows * half)
    weight_bytes = 2 * half * ff

    def shape(*dims, dtype=BF16):
        return jax.ShapeDtypeStruct(dims, dtype)

    near_block, far_block = (planes, 2 * cap, half), (PLANE, 2 * cap, half)

    def exchange(blocks, stride):
        return [blocks[0]] + [
            lax.ppermute(blocks[m], "expert", [(i, i ^ (m * stride)) for i in range(peers)])
            for m in range(1, len(blocks))
        ]

    def regroup(blocks, hold=0):
        outs, *rest = blocks[0].shape
        return call(
            functools.partial(regroup_kernel, len(blocks)),
            tuple(pltpu.HBM((len(blocks), *rest), BF16) for _ in range(outs)),
            (1,),
            [whole(blocks[0].shape)] * len(blocks),
            tuple(whole((len(blocks), *rest)) for _ in range(outs)),
            flops=hold,
            moved=8 * rows * half,
        )(*blocks)

    cuts = (0, quarter, half)
    down_others = [lax.ppermute(w_down[lo:hi], "dp", swap) for lo, hi in zip(cuts, cuts[1:])]
    dy_near = call(
        functools.partial(send_grads_kernel, peers, cap),
        tuple(shape(*near_block) for _ in range(PLANE)),
        (1,),
        [SCALAR, SCALAR, whole(slots_t.shape), whole(route_gates.shape), whole(out_grad.shape)],
        tuple(whole(near_block) for _ in range(PLANE)),
        flops=top * route_flops,
        moved=route_bytes,
    )(group, expert, slots_t, route_gates, out_grad)
    dy_far = regroup(exchange(dy_near, 1))

    tok_send = call(
        functools.partial(send_tokens_kernel, peers, cap),
        shape(2, 2 * rows, quarter),
        (1,),
        [whole(slots_t.shape), whole(tokens.shape)],
        whole((2, 2 * rows, quarter)),
        flops=route_flops,
        moved=route_bytes,
    )(slots_t, tokens)
    tok_recv = lax.all_to_all(
        tok_send.reshape(2 * peers, 2 * cap, quarter), ("dp", "expert"), 0, 0, tiled=True
    ).reshape(2, 2 * rows, quarter)

    part_block = pl.BlockSpec((rows, tile), lambda i: (0, i))
    pair_block = pl.BlockSpec((2, rows, tile), lambda i: (0, 0, i))
    weight_block = pl.BlockSpec((half, tile), lambda i: (0, i))
    quarter_block = pl.BlockSpec((quarter, tile), lambda i: (0, i))
    target, *_ = lax.optimization_barrier((straight[:, None], down_others[0], *dy_far))
    pick = call(
        pick_kernel,
        shape(2 * rows, 2 * rows),
        (1,),
        [whole((2 * rows, 1))],
        whole((2 * rows, 2 * rows)),
        flops=AHEAD_OF_PARTIAL,
        moved=8 * rows * rows,
    )(target)

    def partial(other, dtype, received, hold=0):
        return pl.pallas_call(
            functools.partial(partial_kernel, tile),
            out_shape=shape(2, rows, ff, dtype=dtype),
            grid_spec=pltpu.PrefetchScalarGridSpec(
                num_scalar_prefetch=1,
                grid=(1,),
                in_specs=[
                    whole((2 * rows, 2 * rows)),
                    pl.BlockSpec((1, 2 * rows, quarter), lambda i, g: (other ^ g[0], 0, 0)),
                    HBM,
                    HBM,
                ],
                out_specs=whole((2, rows, ff)),
                scratch_shapes=[
                    pltpu.VMEM((rows, half), BF16),
                    pltpu.VMEM((2, half, ff), BF16),
                    pltpu.SemaphoreType.DMA((2, ff // tile)),
                ],
            ),
            cost_estimate=pl.CostEstimate(
                flops=matmul_flops + hold, bytes_accessed=2 * weight_bytes + 2 * rows * half, transcendentals=0
            ),
            compiler_params=pltpu.CompilerParams(vmem_limit_bytes=24 * 2**20),
        )(
            group,
            pick,
            received,
            pltpu.with_memory_space_constraint(w_gate, pltpu.HBM),
            pltpu.with_memory_space_constraint(w_up, pltpu.HBM),
        )

    part_send = partial(1, BF16, tok_recv)
    part_send, down_others[1] = lax.optimization_barrier((part_send, down_others[1]))
    part_recv = lax.ppermute(part_send, "dp", swap)
    dy_came = exchange(dy_far, PLANE)
    part_mine = partial(0, F32, tok_recv)

    d_hidden, dy_mine, dy_other = call(
        hidden_grad_kernel,
        (shape(rows, ff, dtype=F32), shape(rows, half), shape(rows, half)),
        (ff // tile,),
        [whole((2 * rows, 1)), weight_block] + [quarter_block] * 2 + [whole((PLANE * 2 * cap, half))] * planes,
        (part_block, whole((rows, half)), whole((rows, half))),
        [pltpu.VMEM((2 * rows, half), BF16)],
        flops=matmul_flops + AHEAD_OF_BACKWARD,
        moved=2 * weight_bytes + 4 * rows * half,
    )(moved[:, None], w_down, *down_others, *(came.reshape(PLANE * 2 * cap, half) for came in dy_came))
    hidden, d_pair = call(
        pointwise_kernel,
        (shape(rows, ff), shape(2, rows, ff)),
        (ff // tile,),
        [pair_block, pair_block, part_block],
        (part_block, pair_block),
        flops=20 * rows * ff,
        moved=22 * rows * ff,
    )(part_mine, part_recv, d_hidden)
    y_far = call(
        forward_kernel,
        tuple(shape(*far_block) for _ in range(planes)),
        (1,),
        [whole((1, 2 * rows)), whole((rows, ff)), whole((half, ff))] + [whole((quarter, ff))] * 2,
        tuple(whole(far_block) for _ in range(planes)),
        [pltpu.VMEM((2 * rows, quarter), BF16)],
        flops=matmul_flops,
        moved=2 * weight_bytes + 4 * rows * half,
    )(moved[None, :], hidden, w_down, *down_others)
    hidden_recv = lax.ppermute(hidden, "dp", swap)
    d_recv = lax.ppermute(d_pair, "dp", swap)
    dy_other, _ = lax.optimization_barrier((dy_other, d_pair))
    dy_cross = lax.ppermute(dy_other, "dp", swap)

    *_, d_recv = lax.optimization_barrier((*y_far, d_recv))
    y_far_came = exchange(y_far, PLANE)
    def input_grad(other, d_rows, *before):
        return pl.pallas_call(
            functools.partial(input_grad_kernel, other),
            out_shape=shape(2, 2 * rows, quarter),
            grid_spec=pltpu.PrefetchScalarGridSpec(
                num_scalar_prefetch=1,
                grid=(1,),
                in_specs=[
                    whole((1, 2 * rows)),
                    whole((2, rows, ff)),
                    whole((half, ff)),
                    whole((half, ff)),
                    *[HBM for _ in before],
                ],
                out_specs=pl.BlockSpec((1, 2 * rows, quarter), lambda i, g: (other ^ g[0], 0, 0)),
                scratch_shapes=[pltpu.VMEM((2 * rows, quarter), BF16)],
            ),
            input_output_aliases={5: 0} if before else {},
            cost_estimate=pl.CostEstimate(
                flops=matmul_flops, bytes_accessed=2 * weight_bytes + 2 * rows * half, transcendentals=0
            ),
            compiler_params=pltpu.CompilerParams(vmem_limit_bytes=24 * 2**20),
        )(group, straight[None, :], d_rows, w_gate, w_up, *before)

    dx_send = input_grad(1, d_recv, input_grad(0, d_pair))
    y_far_done = y_far_came
    _, *y_far_came = lax.optimization_barrier((dy_cross, *y_far_came))
    y_near = regroup(y_far_came, AHEAD_OF_REGROUP)
    dx_send, *_ = lax.optimization_barrier((dx_send, y_far_done[2]))
    y_came = exchange(y_near, 1)
    dx_back = lax.all_to_all(
        dx_send.reshape(2 * peers, 2 * cap, quarter), ("dp", "expert"), 0, 0, tiled=True
    ).reshape(2, 2 * rows, quarter)

    strip_block = pl.BlockSpec((rows, narrow), lambda i: (0, i))
    down_grad = call(
        down_kernel,
        shape(half, ff),
        (half // narrow,),
        [strip_block, strip_block, whole((rows, ff)), whole((rows, ff))],
        pl.BlockSpec((narrow, ff), lambda i: (i, 0)),
        flops=matmul_flops,
        moved=weight_bytes + 4 * rows * half,
    )(dy_mine, dy_cross, hidden, hidden_recv)[None]
    moe_out = call(
        functools.partial(combine_out_kernel, peers, cap),
        shape(count, width),
        (1,),
        [SCALAR, SCALAR, whole(route_slot.shape), whole(route_gates.shape)]
        + [whole((planes * 2 * cap, half))] * PLANE,
        whole((count, width)),
        [pltpu.VMEM((2 * rows, half), BF16)],
        flops=top * route_flops,
        moved=route_bytes,
    )(group, expert, route_slot, route_gates, *(came.reshape(planes * 2 * cap, half) for came in y_came))
    token_grad = call(
        functools.partial(combine_grad_kernel, peers, cap),
        shape(count, width),
        (1,),
        [whole(route_slot.shape), whole((2, 2 * rows, quarter))],
        whole((count, width)),
        flops=route_flops,
        moved=route_bytes,
    )(route_slot, dx_back)
    return (moe_out, token_grad, down_grad)


def capacity_of(count, top, peers):
    return max(2, (5 * count * top + 4 * peers - 1) // (4 * peers))


def expert_forward(rows_in, w_gate, w_up, w_down):
    gate_proj = jnp.dot(rows_in, w_gate, preferred_element_type=jnp.float32)
    up_proj = jnp.dot(rows_in, w_up, preferred_element_type=jnp.float32)
    sigma_gate = jax.nn.sigmoid(gate_proj)
    activated = gate_proj * sigma_gate
    hidden = (activated * up_proj).astype(jnp.bfloat16)
    outputs = lax.dot_general(
        hidden, w_down, (((1,), (1,)), ((), ())), preferred_element_type=jnp.float32
    ).astype(jnp.bfloat16)
    return (outputs, gate_proj, up_proj, hidden)


def expert_backward(rows_grad, gate_proj, up_proj, w_gate, w_up, w_down):
    grad_hidden = jnp.dot(rows_grad, w_down, preferred_element_type=jnp.float32)
    sigma_gate = jax.nn.sigmoid(gate_proj)
    activated = gate_proj * sigma_gate
    grad_gate = (
        grad_hidden * up_proj * sigma_gate * (1.0 + gate_proj * (1.0 - sigma_gate))
    ).astype(jnp.bfloat16)
    grad_up = (grad_hidden * activated).astype(jnp.bfloat16)
    contract_dims = (((1,), (1,)), ((), ()))
    summed = lax.dot_general(
        grad_gate, w_gate, contract_dims, preferred_element_type=jnp.float32
    ) + lax.dot_general(grad_up, w_up, contract_dims, preferred_element_type=jnp.float32)
    return summed.astype(jnp.bfloat16)


def gathered_weights(tokens, out_grad, route_gates, route_slot, gate_weight, up_weight, down_weight):
    tok_dev, model_width = tokens.shape
    route_count = route_slot.shape[1]
    peer_count = lax.axis_size("expert")
    capacity = capacity_of(tok_dev, route_count, peer_count)
    route_total = tok_dev * route_count
    send_rows = peer_count * capacity
    flat_slot = route_slot.reshape(-1)
    onehot = (flat_slot[:, None] == jnp.arange(peer_count, dtype=jnp.int32)[None, :]).astype(
        jnp.int32
    )
    slot_rank = jnp.sum((jnp.cumsum(onehot, axis=0) - onehot) * onehot, axis=1)
    send_index = flat_slot * capacity + slot_rank
    route_of_row = (
        jnp.full((send_rows,), route_total, jnp.int32)
        .at[send_index]
        .set(jnp.arange(route_total, dtype=jnp.int32))
    )
    filled = route_of_row < route_total
    safe_route = jnp.where(filled, route_of_row, 0)
    token_row = safe_route // route_count
    gate_value = jnp.where(filled, route_gates.reshape(-1)[safe_route], 0.0)
    rows_in = jnp.where(filled[:, None], tokens[token_row], jnp.zeros((), tokens.dtype))
    rows_in = rows_in.reshape(peer_count, capacity, model_width)
    rows_grad = (gate_value[:, None] * out_grad[token_row].astype(jnp.float32)).astype(jnp.bfloat16)
    rows_grad = rows_grad.reshape(peer_count, capacity, model_width)
    full_gate, full_up, full_down = (
        lax.all_gather(gate_weight, "dp", axis=1, tiled=True),
        lax.all_gather(up_weight, "dp", axis=1, tiled=True),
        lax.all_gather(down_weight, "dp", axis=1, tiled=True),
    )
    w_gate = full_gate[0]
    w_up = full_up[0]
    w_down = full_down[0]
    item_shape = (peer_count, capacity, model_width)
    received = lax.all_to_all(rows_in, "expert", split_axis=0, concat_axis=0, tiled=True)
    outputs, gate_proj, up_proj, hidden_saved = expert_forward(
        received.reshape(-1, model_width), w_gate, w_up, w_down
    )
    out_back = lax.all_to_all(
        outputs.reshape(item_shape), "expert", split_axis=0, concat_axis=0, tiled=True
    )
    grad_in = lax.all_to_all(rows_grad, "expert", split_axis=0, concat_axis=0, tiled=True)
    grad_rows = expert_backward(
        grad_in.reshape(-1, model_width), gate_proj, up_proj, w_gate, w_up, w_down
    )
    grad_back = lax.all_to_all(
        grad_rows.reshape(item_shape), "expert", split_axis=0, concat_axis=0, tiled=True
    )
    grad_flat = grad_in.reshape(-1, model_width)
    down_share = lax.psum_scatter(
        lax.dot_general(
            grad_flat, hidden_saved, (((0,), (0,)), ((), ())), preferred_element_type=jnp.float32
        ).astype(jnp.bfloat16),
        "dp",
        scatter_dimension=0,
        tiled=True,
    )
    down_grad = down_share[None]
    out_routes = out_back.reshape(send_rows, model_width)[send_index].astype(jnp.float32)
    out_routes = out_routes.reshape(tok_dev, route_count, model_width)
    moe_out = jnp.sum(route_gates[:, :, None] * out_routes, axis=1).astype(jnp.bfloat16)
    grad_routes = grad_back.reshape(send_rows, model_width)[send_index].astype(jnp.float32)
    token_grad = jnp.sum(grad_routes.reshape(tok_dev, route_count, model_width), axis=1).astype(
        jnp.bfloat16
    )
    return (moe_out, token_grad, down_grad)


def per_device(tokens, out_grad, route_gates, route_slot, gate_weight, up_weight, down_weight):
    count, _ = tokens.shape
    peers = lax.axis_size("expert")
    cap = capacity_of(count, route_slot.shape[1], peers)
    half, hidden_width = gate_weight.shape[1:]
    fits = (
        lax.axis_size("dp") == 2
        and peers % PLANE == 0
        and peers & (peers - 1) == 0
        and cap % 4 == 0
        and (peers * cap) % 16 == 0
        and count % 128 == 0
        and half % 512 == 0
        and hidden_width % 256 == 0
    )
    plan = split_width if fits else gathered_weights
    return plan(tokens, out_grad, route_gates, route_slot, gate_weight, up_weight, down_weight)


def solution(mesh):
    placed = (
        P(("dp", "expert"), None),
        P(("dp", "expert"), None),
        P(("dp", "expert"), None),
        P(("dp", "expert"), None),
        P("expert", "dp", None),
        P("expert", "dp", None),
        P("expert", "dp", None),
    )
    return jax.shard_map(
        per_device,
        mesh=mesh,
        in_specs=placed,
        out_specs=(P(("dp", "expert"), None), P(("dp", "expert"), None), P("expert", "dp", None)),
        check_vma=False,
    )
```

```python
import functools

import jax
import jax.numpy as jnp
from jax import lax
from jax.experimental import pallas as pl
from jax.experimental.pallas import tpu as pltpu
from jax.sharding import PartitionSpec as P

PLANE = 4
F32, BF16, I32 = jnp.float32, jnp.bfloat16, jnp.int32
NT = (((1,), (1,)), ((), ()))
TN = (((0,), (0,)), ((), ()))


def mm(a, b, dims=(((1,), (0,)), ((), ()))):
    return lax.dot_general(a, b, dims, preferred_element_type=F32)


def ones_where(mask):
    return jnp.where(mask, 1.0, 0.0).astype(BF16)


def iota(shape, dim):
    return lax.broadcasted_iota(I32, shape, dim)


def call(kernel, out_shape, grid, in_specs, out_specs, scratch=(), flops=0, moved=0, vmem_mib=24):
    return pl.pallas_call(
        kernel,
        out_shape=out_shape,
        grid=grid,
        in_specs=in_specs,
        out_specs=out_specs,
        scratch_shapes=list(scratch),
        cost_estimate=pl.CostEstimate(flops=flops, bytes_accessed=moved, transcendentals=0),
        compiler_params=pltpu.CompilerParams(vmem_limit_bytes=vmem_mib * 2**20),
    )


def whole(shape):
    return pl.BlockSpec(shape, lambda *_: (0,) * len(shape))


def column_half(group, half):
    return pl.ds(pl.multiple_of(group * half, 128), half)


AHEAD_OF_PARTIAL, AHEAD_OF_BACKWARD, AHEAD_OF_REGROUP = (int(each) for each in (20e9, 8e9, 20e9))
SCALAR = pl.BlockSpec(memory_space=pltpu.SMEM)
HBM = pl.BlockSpec(memory_space=pltpu.HBM)


def ranks_in_lanes(slots, peers):
    top, count = slots.shape
    named = [jnp.where(iota((peers, count), 0) == slots[k : k + 1, :], 1.0, 0.0) for k in range(top)]
    earlier = ones_where(iota((count, count), 0) < iota((count, count), 1))
    before = mm(sum(named).astype(BF16), earlier)
    return [jnp.sum(before * each, axis=0, keepdims=True).astype(I32) for each in named]


def ranks_in_rows(slots, peers):
    count, top = slots.shape
    named = [jnp.where(iota((count, peers), 1) == slots[:, k : k + 1], 1.0, 0.0) for k in range(top)]
    earlier = ones_where(iota((count, count), 1) < iota((count, count), 0))
    before = mm(earlier, sum(named).astype(BF16))
    return [jnp.sum(before * each, axis=1, keepdims=True).astype(I32) for each in named]


def masks_of(number, expert):
    return (number ^ expert) & (PLANE - 1), (number ^ expert) // PLANE


def spread(values, refs, columns, block):
    each = refs[0].shape[0]
    for m, ref in enumerate(refs):
        for i in range(each):
            lo = (each * m + i) * block
            ref[i, :, columns] = values[lo : lo + block].astype(BF16)


def send_tokens_kernel(peers, cap, slots_ref, tok_ref, out_ref):
    _, rows, width = out_ref.shape
    slots = slots_ref[...]
    at = iota((rows, slots.shape[1]), 0)
    places = [slots[k : k + 1, :] * (2 * cap) + rank for k, rank in enumerate(ranks_in_lanes(slots, peers))]
    halves = [sum(jnp.where(at == place + h * cap, 1.0, 0.0) for place in places) for h in range(2)]
    pick = jnp.concatenate(halves, axis=1).astype(BF16)
    for part in range(2):
        lo = part * 2 * width
        both = jnp.concatenate([tok_ref[:, lo : lo + width], tok_ref[:, lo + width : lo + 2 * width]], axis=0)
        out_ref[part] = mm(pick, both).astype(BF16)


def send_grads_kernel(peers, cap, group_ref, expert_ref, slots_ref, gates_ref, grad_ref, *out_refs):
    slots, gates = slots_ref[...], gates_ref[...]
    group, expert = group_ref[0], expert_ref[0]
    rows, count = 2 * cap * peers, slots.shape[1]
    half = out_refs[0].shape[2]
    at = iota((rows, count), 0)
    halves = [grad_ref[:, column_half(g, half)].astype(F32) for g in (group, 1 - group)]
    total = None
    for k, rank in enumerate(ranks_in_lanes(slots, peers)):
        near, far = masks_of(slots[k : k + 1, :], expert)
        place = (near * (peers // PLANE) + far) * (2 * cap) + rank
        pick = jnp.concatenate([jnp.where(at == place + o * cap, 1.0, 0.0) for o in range(2)], axis=1).astype(BF16)
        both = jnp.concatenate([(gates[:, k : k + 1] * each).astype(BF16) for each in halves], axis=0)
        rows_k = mm(pick, both)
        total = rows_k if total is None else total + rows_k
    spread(total, out_refs, slice(None), 2 * cap)


def halve_kernel(pieces, from_ref, *refs):
    *out_refs, held_ref, sems = refs
    size = out_refs[0].shape[0] // pieces
    parts = [(i, p, pl.ds((i * pieces + p) * size, size)) for i in range(2) for p in range(pieces)]
    arrive = [pltpu.make_async_copy(from_ref.at[at], held_ref.at[at], sems.at[0, i, p]) for i, p, at in parts]
    leave = [
        pltpu.make_async_copy(held_ref.at[at], out_refs[i].at[pl.ds(p * size, size)], sems.at[1, i, p])
        for i, p, at in parts
    ]
    for copy in arrive:
        copy.start()
    for came, copy in zip(arrive, leave):
        came.wait()
        copy.start()
    for copy in leave:
        copy.wait()


def regroup_kernel(count, *refs):
    blocks, outs = refs[:count], refs[count:]
    for i, out_ref in enumerate(outs):
        for m, block_ref in enumerate(blocks):
            out_ref[m] = block_ref[i]


def pick_kernel(target_ref, out_ref):
    out_ref[...] = ones_where(iota(out_ref.shape, 1) == target_ref[...])


def partial_kernel(tile, group_ref, pick_ref, recv_ref, wg_ref, wu_ref, out_ref, x_ref, w_ref, sems):
    _, rows, ff = out_ref.shape
    width = recv_ref.shape[2]
    copies = {}
    for t in range(ff // tile):
        columns = pl.ds(t * tile, tile)
        for i, ref in enumerate((wg_ref, wu_ref)):
            copies[t, i] = pltpu.make_async_copy(ref.at[:, columns], w_ref.at[i, :, columns], sems.at[i, t])
            copies[t, i].start()
    for h in range(2):
        x_ref[:, h * width : (h + 1) * width] = mm(pick_ref[h * rows : (h + 1) * rows, :], recv_ref[0]).astype(BF16)
    for t in range(ff // tile):
        columns = slice(t * tile, (t + 1) * tile)
        for i in range(2):
            copies[t, i].wait()
            out_ref[i, :, columns] = mm(x_ref[...], w_ref[i, :, columns]).astype(out_ref.dtype)


def hidden_grad_kernel(target_ref, own_ref, other_0_ref, other_1_ref, *refs):
    *came_refs, out_ref, dy_mine_ref, dy_send_ref, came_ref = refs
    rows = out_ref.shape[0]

    @pl.when(pl.program_id(0) == 0)
    def _():
        each = came_refs[0].shape[0]
        for m, ref in enumerate(came_refs):
            came_ref[m * each : (m + 1) * each, :] = ref[...]
        pick = ones_where(iota((2 * rows, 2 * rows), 1) == target_ref[...])
        dy = mm(pick, came_ref[...]).astype(BF16)
        dy_mine_ref[...] = dy[:rows]
        dy_send_ref[...] = dy[rows:]

    cut = other_0_ref.shape[0]
    total = mm(dy_mine_ref[...], own_ref[...])
    total = total + mm(dy_send_ref[:, :cut], other_0_ref[...])
    out_ref[...] = total + mm(dy_send_ref[:, cut:], other_1_ref[...])


def pointwise_kernel(mine_ref, recv_ref, d_hidden_ref, hid_ref, out_ref):
    gate = mine_ref[0] + recv_ref[0].astype(F32)
    up = mine_ref[1] + recv_ref[1].astype(F32)
    sigma = jax.nn.sigmoid(gate)
    active = gate * sigma
    d_hidden = d_hidden_ref[...]
    out_ref[0] = (d_hidden * up * sigma * (1.0 + gate * (1.0 - sigma))).astype(BF16)
    out_ref[1] = (d_hidden * active).astype(BF16)
    hid_ref[...] = (active * up).astype(BF16)


def forward_kernel(target_ref, hid_ref, own_ref, other_0_ref, other_1_ref, *refs):
    *out_refs, y_ref = refs
    rows = hid_ref.shape[0]
    cut = other_0_ref.shape[0]
    pick = ones_where(iota((2 * rows, 2 * rows), 0) == target_ref[...])
    for i, other_ref in enumerate((other_0_ref, other_1_ref)):
        columns = slice(i * cut, (i + 1) * cut)
        y_ref[:rows, :] = mm(hid_ref[...], own_ref[columns, :], NT).astype(BF16)
        y_ref[rows:, :] = mm(hid_ref[...], other_ref[...], NT).astype(BF16)
        spread(mm(pick, y_ref[...]), out_refs, columns, out_refs[0].shape[1])


def input_grad_kernel(other, group_ref, target_ref, d_ref, wg_ref, wu_ref, *refs):
    *_, out_ref, dx_ref = refs
    rows = d_ref.shape[1]
    width = out_ref.shape[2]
    for h in range(2):
        part = slice(h * width, (h + 1) * width)
        dx = mm(d_ref[0], wg_ref[part, :], NT) + mm(d_ref[1], wu_ref[part, :], NT)
        dx_ref[h * rows : (h + 1) * rows, :] = dx.astype(BF16)
    pick = ones_where(iota((2 * rows, 2 * rows), 0) == target_ref[...])
    out_ref[0] = mm(pick, dx_ref[...]).astype(BF16)


def down_kernel(mine_ref, recv_ref, hid_ref, hid_recv_ref, out_ref):
    out_ref[...] = (mm(mine_ref[...], hid_ref[...], TN) + mm(recv_ref[...], hid_recv_ref[...], TN)).astype(BF16)


def combine_out_kernel(peers, cap, group_ref, expert_ref, slots_ref, gates_ref, *refs):
    *came_refs, out_ref, came_ref = refs
    slots, gates = slots_ref[...], gates_ref[...]
    group, expert = group_ref[0], expert_ref[0]
    rows, half = came_ref.shape
    each = rows // len(came_refs)
    for m, ref in enumerate(came_refs):
        came_ref[m * each : (m + 1) * each, :] = ref[...]
    at = iota((slots.shape[0], rows), 1)
    places = []
    for k, rank in enumerate(ranks_in_rows(slots, peers)):
        near, far = masks_of(slots[:, k : k + 1], expert)
        places.append((near * (peers // PLANE) + far) * (2 * cap) + rank)
    for o, g in enumerate((group, 1 - group)):
        total = None
        for k, place in enumerate(places):
            term = gates[:, k : k + 1] * mm(ones_where(at == place + o * cap), came_ref[...])
            total = term if total is None else total + term
        out_ref[:, column_half(g, half)] = total.astype(BF16)


def combine_grad_kernel(peers, cap, slots_ref, back_ref, out_ref):
    slots = slots_ref[...]
    places = [slots[:, k : k + 1] * (2 * cap) + rank for k, rank in enumerate(ranks_in_rows(slots, peers))]
    _, rows, width = back_ref.shape
    at = iota((slots.shape[0], rows), 1)
    for h in range(2):
        pick = sum(jnp.where(at == place + h * cap, 1.0, 0.0) for place in places).astype(BF16)
        for part in range(2):
            lo = (2 * part + h) * width
            out_ref[:, lo : lo + width] = mm(pick, back_ref[part]).astype(BF16)


def split_width(tokens, out_grad, route_gates, route_slot, gate_weight, up_weight, down_weight):
    count, width = tokens.shape
    top = route_slot.shape[1]
    peers = lax.axis_size("expert")
    planes = peers // PLANE
    cap = capacity_of(count, top, peers)
    w_gate, w_up, w_down = gate_weight[0], up_weight[0], down_weight[0]
    half, ff = w_gate.shape
    quarter = half // 2
    rows = peers * cap
    swap = [(0, 1), (1, 0)]
    index = lax.axis_index("dp").astype(I32)
    group, expert = index.reshape(1), lax.axis_index("expert").astype(I32).reshape(1)
    slots_t = route_slot.T
    place = jnp.arange(rows, dtype=I32)
    straight_left = (place // cap) * (2 * cap) + place % cap
    straight = jnp.concatenate([straight_left, straight_left + cap])
    near, far = masks_of(place // cap, expert)
    moved_left = (far * PLANE + near) * (2 * cap) + place % cap
    moved = jnp.concatenate([moved_left, moved_left + cap])
    tile, narrow = min(256, ff), min(256, half)
    matmul_flops = 2 * 2 * rows * half * ff
    route_flops = 2 * 2 * rows * 2 * count * half
    route_bytes = 2 * (tokens.size + 2 * rows * half)
    weight_bytes = 2 * half * ff

    def shape(*dims, dtype=BF16):
        return jax.ShapeDtypeStruct(dims, dtype)

    near_block, far_block = (planes, 2 * cap, half), (PLANE, 2 * cap, half)

    def exchange(blocks, stride):
        return [blocks[0]] + [
            lax.ppermute(blocks[m], "expert", [(i, i ^ (m * stride)) for i in range(peers)])
            for m in range(1, len(blocks))
        ]

    def regroup(blocks, hold=0):
        outs, *rest = blocks[0].shape
        return call(
            functools.partial(regroup_kernel, len(blocks)),
            tuple(pltpu.HBM((len(blocks), *rest), BF16) for _ in range(outs)),
            (1,),
            [whole(blocks[0].shape)] * len(blocks),
            tuple(whole((len(blocks), *rest)) for _ in range(outs)),
            flops=hold,
            moved=8 * rows * half,
        )(*blocks)

    pieces = 4
    down_halves = call(
        functools.partial(halve_kernel, pieces),
        tuple(pltpu.HBM((quarter, ff), BF16) for _ in range(2)),
        (1,),
        [HBM],
        (HBM, HBM),
        [pltpu.VMEM((half, ff), BF16), pltpu.SemaphoreType.DMA((2, 2, pieces))],
        moved=2 * weight_bytes,
    )(pltpu.with_memory_space_constraint(w_down, pltpu.HBM))
    down_others = [lax.ppermute(each, "dp", swap) for each in down_halves]
    dy_near = call(
        functools.partial(send_grads_kernel, peers, cap),
        tuple(shape(*near_block) for _ in range(PLANE)),
        (1,),
        [SCALAR, SCALAR, whole(slots_t.shape), whole(route_gates.shape), whole(out_grad.shape)],
        tuple(whole(near_block) for _ in range(PLANE)),
        flops=top * route_flops,
        moved=route_bytes,
    )(group, expert, slots_t, route_gates, out_grad)
    dy_far = regroup(exchange(dy_near, 1))

    tok_send = call(
        functools.partial(send_tokens_kernel, peers, cap),
        shape(2, 2 * rows, quarter),
        (1,),
        [whole(slots_t.shape), whole(tokens.shape)],
        whole((2, 2 * rows, quarter)),
        flops=route_flops,
        moved=route_bytes,
    )(slots_t, tokens)
    tok_recv = lax.all_to_all(
        tok_send.reshape(2 * peers, 2 * cap, quarter), ("dp", "expert"), 0, 0, tiled=True
    ).reshape(2, 2 * rows, quarter)

    part_block = pl.BlockSpec((rows, tile), lambda i: (0, i))
    pair_block = pl.BlockSpec((2, rows, tile), lambda i: (0, 0, i))
    weight_block = pl.BlockSpec((half, tile), lambda i: (0, i))
    quarter_block = pl.BlockSpec((quarter, tile), lambda i: (0, i))
    target, *_ = lax.optimization_barrier((straight[:, None], down_others[0], *dy_far))
    pick = call(
        pick_kernel,
        shape(2 * rows, 2 * rows),
        (1,),
        [whole((2 * rows, 1))],
        whole((2 * rows, 2 * rows)),
        flops=AHEAD_OF_PARTIAL,
        moved=8 * rows * rows,
    )(target)

    def partial(other, dtype, received, hold=0):
        return pl.pallas_call(
            functools.partial(partial_kernel, tile),
            out_shape=shape(2, rows, ff, dtype=dtype),
            grid_spec=pltpu.PrefetchScalarGridSpec(
                num_scalar_prefetch=1,
                grid=(1,),
                in_specs=[
                    whole((2 * rows, 2 * rows)),
                    pl.BlockSpec((1, 2 * rows, quarter), lambda i, g: (other ^ g[0], 0, 0)),
                    HBM,
                    HBM,
                ],
                out_specs=whole((2, rows, ff)),
                scratch_shapes=[
                    pltpu.VMEM((rows, half), BF16),
                    pltpu.VMEM((2, half, ff), BF16),
                    pltpu.SemaphoreType.DMA((2, ff // tile)),
                ],
            ),
            cost_estimate=pl.CostEstimate(
                flops=matmul_flops + hold, bytes_accessed=2 * weight_bytes + 2 * rows * half, transcendentals=0
            ),
            compiler_params=pltpu.CompilerParams(vmem_limit_bytes=24 * 2**20),
        )(
            group,
            pick,
            received,
            pltpu.with_memory_space_constraint(w_gate, pltpu.HBM),
            pltpu.with_memory_space_constraint(w_up, pltpu.HBM),
        )

    part_send = partial(1, BF16, tok_recv)
    part_send, down_others[1] = lax.optimization_barrier((part_send, down_others[1]))
    part_recv = lax.ppermute(part_send, "dp", swap)
    dy_came = exchange(dy_far, PLANE)
    part_mine = partial(0, F32, tok_recv)

    d_hidden, dy_mine, dy_other = call(
        hidden_grad_kernel,
        (shape(rows, ff, dtype=F32), shape(rows, half), shape(rows, half)),
        (ff // tile,),
        [whole((2 * rows, 1)), weight_block] + [quarter_block] * 2 + [whole((PLANE * 2 * cap, half))] * planes,
        (part_block, whole((rows, half)), whole((rows, half))),
        [pltpu.VMEM((2 * rows, half), BF16)],
        flops=matmul_flops + AHEAD_OF_BACKWARD,
        moved=2 * weight_bytes + 4 * rows * half,
    )(moved[:, None], w_down, *down_others, *(came.reshape(PLANE * 2 * cap, half) for came in dy_came))
    hidden, d_pair = call(
        pointwise_kernel,
        (shape(rows, ff), shape(2, rows, ff)),
        (ff // tile,),
        [pair_block, pair_block, part_block],
        (part_block, pair_block),
        flops=20 * rows * ff,
        moved=22 * rows * ff,
    )(part_mine, part_recv, d_hidden)
    y_far = call(
        forward_kernel,
        tuple(shape(*far_block) for _ in range(planes)),
        (1,),
        [whole((1, 2 * rows)), whole((rows, ff)), whole((half, ff))] + [whole((quarter, ff))] * 2,
        tuple(whole(far_block) for _ in range(planes)),
        [pltpu.VMEM((2 * rows, quarter), BF16)],
        flops=matmul_flops,
        moved=2 * weight_bytes + 4 * rows * half,
    )(moved[None, :], hidden, w_down, *down_others)
    hidden_recv = lax.ppermute(hidden, "dp", swap)
    d_recv = lax.ppermute(d_pair, "dp", swap)
    dy_other, _ = lax.optimization_barrier((dy_other, d_pair))
    dy_cross = lax.ppermute(dy_other, "dp", swap)

    *_, d_recv = lax.optimization_barrier((*y_far, d_recv))
    y_far_came = exchange(y_far, PLANE)
    def input_grad(other, d_rows, *before):
        return pl.pallas_call(
            functools.partial(input_grad_kernel, other),
            out_shape=shape(2, 2 * rows, quarter),
            grid_spec=pltpu.PrefetchScalarGridSpec(
                num_scalar_prefetch=1,
                grid=(1,),
                in_specs=[
                    whole((1, 2 * rows)),
                    whole((2, rows, ff)),
                    whole((half, ff)),
                    whole((half, ff)),
                    *[HBM for _ in before],
                ],
                out_specs=pl.BlockSpec((1, 2 * rows, quarter), lambda i, g: (other ^ g[0], 0, 0)),
                scratch_shapes=[pltpu.VMEM((2 * rows, quarter), BF16)],
            ),
            input_output_aliases={5: 0} if before else {},
            cost_estimate=pl.CostEstimate(
                flops=matmul_flops, bytes_accessed=2 * weight_bytes + 2 * rows * half, transcendentals=0
            ),
            compiler_params=pltpu.CompilerParams(vmem_limit_bytes=24 * 2**20),
        )(group, straight[None, :], d_rows, w_gate, w_up, *before)

    dx_send = input_grad(1, d_recv, input_grad(0, d_pair))
    y_far_done = y_far_came
    _, *y_far_came = lax.optimization_barrier((dy_cross, *y_far_came))
    y_near = regroup(y_far_came, AHEAD_OF_REGROUP)
    dx_send, *_ = lax.optimization_barrier((dx_send, y_far_done[2]))
    y_came = exchange(y_near, 1)
    dx_back = lax.all_to_all(
        dx_send.reshape(2 * peers, 2 * cap, quarter), ("dp", "expert"), 0, 0, tiled=True
    ).reshape(2, 2 * rows, quarter)

    strip_block = pl.BlockSpec((rows, narrow), lambda i: (0, i))
    down_grad = call(
        down_kernel,
        shape(half, ff),
        (half // narrow,),
        [strip_block, strip_block, whole((rows, ff)), whole((rows, ff))],
        pl.BlockSpec((narrow, ff), lambda i: (i, 0)),
        flops=matmul_flops,
        moved=weight_bytes + 4 * rows * half,
    )(dy_mine, dy_cross, hidden, hidden_recv)[None]
    moe_out = call(
        functools.partial(combine_out_kernel, peers, cap),
        shape(count, width),
        (1,),
        [SCALAR, SCALAR, whole(route_slot.shape), whole(route_gates.shape)]
        + [whole((planes * 2 * cap, half))] * PLANE,
        whole((count, width)),
        [pltpu.VMEM((2 * rows, half), BF16)],
        flops=top * route_flops,
        moved=route_bytes,
    )(group, expert, route_slot, route_gates, *(came.reshape(planes * 2 * cap, half) for came in y_came))
    token_grad = call(
        functools.partial(combine_grad_kernel, peers, cap),
        shape(count, width),
        (1,),
        [whole(route_slot.shape), whole((2, 2 * rows, quarter))],
        whole((count, width)),
        flops=route_flops,
        moved=route_bytes,
    )(route_slot, dx_back)
    return (moe_out, token_grad, down_grad)


def capacity_of(count, top, peers):
    return max(2, (5 * count * top + 4 * peers - 1) // (4 * peers))


def expert_forward(rows_in, w_gate, w_up, w_down):
    gate_proj = jnp.dot(rows_in, w_gate, preferred_element_type=jnp.float32)
    up_proj = jnp.dot(rows_in, w_up, preferred_element_type=jnp.float32)
    sigma_gate = jax.nn.sigmoid(gate_proj)
    activated = gate_proj * sigma_gate
    hidden = (activated * up_proj).astype(jnp.bfloat16)
    outputs = lax.dot_general(
        hidden, w_down, (((1,), (1,)), ((), ())), preferred_element_type=jnp.float32
    ).astype(jnp.bfloat16)
    return (outputs, gate_proj, up_proj, hidden)


def expert_backward(rows_grad, gate_proj, up_proj, w_gate, w_up, w_down):
    grad_hidden = jnp.dot(rows_grad, w_down, preferred_element_type=jnp.float32)
    sigma_gate = jax.nn.sigmoid(gate_proj)
    activated = gate_proj * sigma_gate
    grad_gate = (
        grad_hidden * up_proj * sigma_gate * (1.0 + gate_proj * (1.0 - sigma_gate))
    ).astype(jnp.bfloat16)
    grad_up = (grad_hidden * activated).astype(jnp.bfloat16)
    contract_dims = (((1,), (1,)), ((), ()))
    summed = lax.dot_general(
        grad_gate, w_gate, contract_dims, preferred_element_type=jnp.float32
    ) + lax.dot_general(grad_up, w_up, contract_dims, preferred_element_type=jnp.float32)
    return summed.astype(jnp.bfloat16)


def gathered_weights(tokens, out_grad, route_gates, route_slot, gate_weight, up_weight, down_weight):
    tok_dev, model_width = tokens.shape
    route_count = route_slot.shape[1]
    peer_count = lax.axis_size("expert")
    capacity = capacity_of(tok_dev, route_count, peer_count)
    route_total = tok_dev * route_count
    send_rows = peer_count * capacity
    flat_slot = route_slot.reshape(-1)
    onehot = (flat_slot[:, None] == jnp.arange(peer_count, dtype=jnp.int32)[None, :]).astype(
        jnp.int32
    )
    slot_rank = jnp.sum((jnp.cumsum(onehot, axis=0) - onehot) * onehot, axis=1)
    send_index = flat_slot * capacity + slot_rank
    route_of_row = (
        jnp.full((send_rows,), route_total, jnp.int32)
        .at[send_index]
        .set(jnp.arange(route_total, dtype=jnp.int32))
    )
    filled = route_of_row < route_total
    safe_route = jnp.where(filled, route_of_row, 0)
    token_row = safe_route // route_count
    gate_value = jnp.where(filled, route_gates.reshape(-1)[safe_route], 0.0)
    rows_in = jnp.where(filled[:, None], tokens[token_row], jnp.zeros((), tokens.dtype))
    rows_in = rows_in.reshape(peer_count, capacity, model_width)
    rows_grad = (gate_value[:, None] * out_grad[token_row].astype(jnp.float32)).astype(jnp.bfloat16)
    rows_grad = rows_grad.reshape(peer_count, capacity, model_width)
    full_gate, full_up, full_down = (
        lax.all_gather(gate_weight, "dp", axis=1, tiled=True),
        lax.all_gather(up_weight, "dp", axis=1, tiled=True),
        lax.all_gather(down_weight, "dp", axis=1, tiled=True),
    )
    w_gate = full_gate[0]
    w_up = full_up[0]
    w_down = full_down[0]
    item_shape = (peer_count, capacity, model_width)
    received = lax.all_to_all(rows_in, "expert", split_axis=0, concat_axis=0, tiled=True)
    outputs, gate_proj, up_proj, hidden_saved = expert_forward(
        received.reshape(-1, model_width), w_gate, w_up, w_down
    )
    out_back = lax.all_to_all(
        outputs.reshape(item_shape), "expert", split_axis=0, concat_axis=0, tiled=True
    )
    grad_in = lax.all_to_all(rows_grad, "expert", split_axis=0, concat_axis=0, tiled=True)
    grad_rows = expert_backward(
        grad_in.reshape(-1, model_width), gate_proj, up_proj, w_gate, w_up, w_down
    )
    grad_back = lax.all_to_all(
        grad_rows.reshape(item_shape), "expert", split_axis=0, concat_axis=0, tiled=True
    )
    grad_flat = grad_in.reshape(-1, model_width)
    down_share = lax.psum_scatter(
        lax.dot_general(
            grad_flat, hidden_saved, (((0,), (0,)), ((), ())), preferred_element_type=jnp.float32
        ).astype(jnp.bfloat16),
        "dp",
        scatter_dimension=0,
        tiled=True,
    )
    down_grad = down_share[None]
    out_routes = out_back.reshape(send_rows, model_width)[send_index].astype(jnp.float32)
    out_routes = out_routes.reshape(tok_dev, route_count, model_width)
    moe_out = jnp.sum(route_gates[:, :, None] * out_routes, axis=1).astype(jnp.bfloat16)
    grad_routes = grad_back.reshape(send_rows, model_width)[send_index].astype(jnp.float32)
    token_grad = jnp.sum(grad_routes.reshape(tok_dev, route_count, model_width), axis=1).astype(
        jnp.bfloat16
    )
    return (moe_out, token_grad, down_grad)


def per_device(tokens, out_grad, route_gates, route_slot, gate_weight, up_weight, down_weight):
    count, _ = tokens.shape
    peers = lax.axis_size("expert")
    cap = capacity_of(count, route_slot.shape[1], peers)
    half, hidden_width = gate_weight.shape[1:]
    fits = (
        lax.axis_size("dp") == 2
        and peers % PLANE == 0
        and peers & (peers - 1) == 0
        and cap % 4 == 0
        and (peers * cap) % 16 == 0
        and count % 128 == 0
        and half % 512 == 0
        and hidden_width % 256 == 0
    )
    plan = split_width if fits else gathered_weights
    return plan(tokens, out_grad, route_gates, route_slot, gate_weight, up_weight, down_weight)


def solution(mesh):
    placed = (
        P(("dp", "expert"), None),
        P(("dp", "expert"), None),
        P(("dp", "expert"), None),
        P(("dp", "expert"), None),
        P("expert", "dp", None),
        P("expert", "dp", None),
        P("expert", "dp", None),
    )
    return jax.shard_map(
        per_device,
        mesh=mesh,
        in_specs=placed,
        out_specs=(P(("dp", "expert"), None), P(("dp", "expert"), None), P("expert", "dp", None)),
        check_vma=False,
    )
```

```python
import functools

import jax
import jax.numpy as jnp
from jax import lax
from jax.experimental import pallas as pl
from jax.experimental.pallas import tpu as pltpu
from jax.sharding import PartitionSpec as P

PLANE = 4
F32, BF16, I32 = jnp.float32, jnp.bfloat16, jnp.int32
NT = (((1,), (1,)), ((), ()))
TN = (((0,), (0,)), ((), ()))


def mm(a, b, dims=(((1,), (0,)), ((), ()))):
    return lax.dot_general(a, b, dims, preferred_element_type=F32)


def ones_where(mask):
    return jnp.where(mask, 1.0, 0.0).astype(BF16)


def iota(shape, dim):
    return lax.broadcasted_iota(I32, shape, dim)


def call(kernel, out_shape, grid, in_specs, out_specs, scratch=(), flops=0, moved=0, vmem_mib=24):
    return pl.pallas_call(
        kernel,
        out_shape=out_shape,
        grid=grid,
        in_specs=in_specs,
        out_specs=out_specs,
        scratch_shapes=list(scratch),
        cost_estimate=pl.CostEstimate(flops=flops, bytes_accessed=moved, transcendentals=0),
        compiler_params=pltpu.CompilerParams(vmem_limit_bytes=vmem_mib * 2**20),
    )


def whole(shape):
    return pl.BlockSpec(shape, lambda *_: (0,) * len(shape))


def column_half(group, half):
    return pl.ds(pl.multiple_of(group * half, 128), half)


AHEAD_OF_PARTIAL, AHEAD_OF_BACKWARD, AHEAD_OF_REGROUP = (int(each) for each in (20e9, 8e9, 20e9))
SCALAR = pl.BlockSpec(memory_space=pltpu.SMEM)
HBM = pl.BlockSpec(memory_space=pltpu.HBM)


def ranks_in_lanes(slots, peers):
    top, count = slots.shape
    named = [jnp.where(iota((peers, count), 0) == slots[k : k + 1, :], 1.0, 0.0) for k in range(top)]
    earlier = ones_where(iota((count, count), 0) < iota((count, count), 1))
    before = mm(sum(named).astype(BF16), earlier)
    return [jnp.sum(before * each, axis=0, keepdims=True).astype(I32) for each in named]


def ranks_in_rows(slots, peers):
    count, top = slots.shape
    named = [jnp.where(iota((count, peers), 1) == slots[:, k : k + 1], 1.0, 0.0) for k in range(top)]
    earlier = ones_where(iota((count, count), 1) < iota((count, count), 0))
    before = mm(earlier, sum(named).astype(BF16))
    return [jnp.sum(before * each, axis=1, keepdims=True).astype(I32) for each in named]


def masks_of(number, expert):
    return (number ^ expert) & (PLANE - 1), (number ^ expert) // PLANE


def spread(values, refs, columns, block):
    each = refs[0].shape[0]
    for m, ref in enumerate(refs):
        for i in range(each):
            lo = (each * m + i) * block
            ref[i, :, columns] = values[lo : lo + block].astype(BF16)


def send_tokens_kernel(peers, cap, slots_ref, tok_ref, out_ref):
    _, rows, width = out_ref.shape
    slots = slots_ref[...]
    at = iota((rows, slots.shape[1]), 0)
    places = [slots[k : k + 1, :] * (2 * cap) + rank for k, rank in enumerate(ranks_in_lanes(slots, peers))]
    halves = [sum(jnp.where(at == place + h * cap, 1.0, 0.0) for place in places) for h in range(2)]
    pick = jnp.concatenate(halves, axis=1).astype(BF16)
    for part in range(2):
        lo = part * 2 * width
        both = jnp.concatenate([tok_ref[:, lo : lo + width], tok_ref[:, lo + width : lo + 2 * width]], axis=0)
        out_ref[part] = mm(pick, both).astype(BF16)


def send_grads_kernel(peers, cap, group_ref, expert_ref, slots_ref, gates_ref, grad_ref, *out_refs):
    slots, gates = slots_ref[...], gates_ref[...]
    group, expert = group_ref[0], expert_ref[0]
    rows, count = 2 * cap * peers, slots.shape[1]
    half = out_refs[0].shape[2]
    at = iota((rows, count), 0)
    halves = [grad_ref[:, column_half(g, half)].astype(F32) for g in (group, 1 - group)]
    total = None
    for k, rank in enumerate(ranks_in_lanes(slots, peers)):
        near, far = masks_of(slots[k : k + 1, :], expert)
        place = (near * (peers // PLANE) + far) * (2 * cap) + rank
        pick = jnp.concatenate([jnp.where(at == place + o * cap, 1.0, 0.0) for o in range(2)], axis=1).astype(BF16)
        both = jnp.concatenate([(gates[:, k : k + 1] * each).astype(BF16) for each in halves], axis=0)
        rows_k = mm(pick, both)
        total = rows_k if total is None else total + rows_k
    spread(total, out_refs, slice(None), 2 * cap)


def halve_kernel(pieces, from_ref, *refs):
    *out_refs, held_ref, sems = refs
    size = out_refs[0].shape[0] // pieces
    parts = [(i, p, pl.ds((i * pieces + p) * size, size)) for i in range(2) for p in range(pieces)]
    arrive = [pltpu.make_async_copy(from_ref.at[at], held_ref.at[at], sems.at[0, i, p]) for i, p, at in parts]
    leave = [
        pltpu.make_async_copy(held_ref.at[at], out_refs[i].at[pl.ds(p * size, size)], sems.at[1, i, p])
        for i, p, at in parts
    ]
    for copy in arrive:
        copy.start()
    for came, copy in zip(arrive, leave):
        came.wait()
        copy.start()
    for copy in leave:
        copy.wait()


def regroup_kernel(count, *refs):
    blocks, outs = refs[:count], refs[count:]
    for i, out_ref in enumerate(outs):
        for m, block_ref in enumerate(blocks):
            out_ref[m] = block_ref[i]


def pick_kernel(target_ref, out_ref):
    out_ref[...] = ones_where(iota(out_ref.shape, 1) == target_ref[...])


def partial_kernel(tile, group_ref, pick_ref, recv_ref, wg_ref, wu_ref, out_ref, x_ref, w_ref, sems):
    _, rows, ff = out_ref.shape
    width = recv_ref.shape[2]
    copies = {}
    for t in range(ff // tile):
        columns = pl.ds(t * tile, tile)
        for i, ref in enumerate((wg_ref, wu_ref)):
            copies[t, i] = pltpu.make_async_copy(ref.at[:, columns], w_ref.at[i, :, columns], sems.at[i, t])
            copies[t, i].start()
    for h in range(2):
        x_ref[:, h * width : (h + 1) * width] = mm(pick_ref[h * rows : (h + 1) * rows, :], recv_ref[0]).astype(BF16)
    for t in range(ff // tile):
        columns = slice(t * tile, (t + 1) * tile)
        for i in range(2):
            copies[t, i].wait()
            out_ref[i, :, columns] = mm(x_ref[...], w_ref[i, :, columns]).astype(out_ref.dtype)


def hidden_grad_kernel(target_ref, own_ref, other_0_ref, other_1_ref, *refs):
    *came_refs, out_ref, dy_mine_ref, dy_send_ref, came_ref = refs
    rows = out_ref.shape[0]

    @pl.when(pl.program_id(0) == 0)
    def _():
        each = came_refs[0].shape[0]
        for m, ref in enumerate(came_refs):
            came_ref[m * each : (m + 1) * each, :] = ref[...]
        pick = ones_where(iota((2 * rows, 2 * rows), 1) == target_ref[...])
        dy = mm(pick, came_ref[...]).astype(BF16)
        dy_mine_ref[...] = dy[:rows]
        dy_send_ref[...] = dy[rows:]

    cut = other_0_ref.shape[0]
    total = mm(dy_mine_ref[...], own_ref[...])
    total = total + mm(dy_send_ref[:, :cut], other_0_ref[...])
    out_ref[...] = total + mm(dy_send_ref[:, cut:], other_1_ref[...])


def pointwise_kernel(mine_ref, recv_ref, d_hidden_ref, hid_ref, out_ref):
    gate = mine_ref[0] + recv_ref[0].astype(F32)
    up = mine_ref[1] + recv_ref[1].astype(F32)
    sigma = jax.nn.sigmoid(gate)
    active = gate * sigma
    d_hidden = d_hidden_ref[...]
    out_ref[0] = (d_hidden * up * sigma * (1.0 + gate * (1.0 - sigma))).astype(BF16)
    out_ref[1] = (d_hidden * active).astype(BF16)
    hid_ref[...] = (active * up).astype(BF16)


def forward_kernel(target_ref, hid_ref, own_ref, other_0_ref, other_1_ref, *refs):
    *out_refs, y_ref = refs
    rows = hid_ref.shape[0]
    cut = other_0_ref.shape[0]
    pick = ones_where(iota((2 * rows, 2 * rows), 0) == target_ref[...])
    for i, other_ref in enumerate((other_0_ref, other_1_ref)):
        columns = slice(i * cut, (i + 1) * cut)
        y_ref[:rows, :] = mm(hid_ref[...], own_ref[columns, :], NT).astype(BF16)
        y_ref[rows:, :] = mm(hid_ref[...], other_ref[...], NT).astype(BF16)
        spread(mm(pick, y_ref[...]), out_refs, columns, out_refs[0].shape[1])


def input_grad_kernel(other, group_ref, target_ref, d_ref, wg_ref, wu_ref, *refs):
    *_, out_ref, dx_ref = refs
    rows = d_ref.shape[1]
    width = out_ref.shape[2]
    for h in range(2):
        part = slice(h * width, (h + 1) * width)
        dx = mm(d_ref[0], wg_ref[part, :], NT) + mm(d_ref[1], wu_ref[part, :], NT)
        dx_ref[h * rows : (h + 1) * rows, :] = dx.astype(BF16)
    pick = ones_where(iota((2 * rows, 2 * rows), 0) == target_ref[...])
    out_ref[0] = mm(pick, dx_ref[...]).astype(BF16)


def down_kernel(mine_ref, recv_ref, hid_ref, hid_recv_ref, out_ref):
    out_ref[...] = (mm(mine_ref[...], hid_ref[...], TN) + mm(recv_ref[...], hid_recv_ref[...], TN)).astype(BF16)


def combine_out_kernel(peers, cap, group_ref, expert_ref, slots_ref, gates_ref, *refs):
    *came_refs, out_ref, came_ref = refs
    slots, gates = slots_ref[...], gates_ref[...]
    group, expert = group_ref[0], expert_ref[0]
    rows, half = came_ref.shape
    each = rows // len(came_refs)
    for m, ref in enumerate(came_refs):
        came_ref[m * each : (m + 1) * each, :] = ref[...]
    at = iota((slots.shape[0], rows), 1)
    places = []
    for k, rank in enumerate(ranks_in_rows(slots, peers)):
        near, far = masks_of(slots[:, k : k + 1], expert)
        places.append((near * (peers // PLANE) + far) * (2 * cap) + rank)
    count, top = slots.shape
    picks = jnp.concatenate([ones_where(at == place + o * cap) for o in range(2) for place in places], axis=0)
    found = mm(picks, came_ref[...])
    for o, g in enumerate((group, 1 - group)):
        total = None
        for k in range(top):
            lo = (o * top + k) * count
            term = gates[:, k : k + 1] * found[lo : lo + count]
            total = term if total is None else total + term
        out_ref[:, column_half(g, half)] = total.astype(BF16)


def combine_grad_kernel(peers, cap, slots_ref, back_ref, out_ref):
    slots = slots_ref[...]
    places = [slots[:, k : k + 1] * (2 * cap) + rank for k, rank in enumerate(ranks_in_rows(slots, peers))]
    _, rows, width = back_ref.shape
    count = slots.shape[0]
    at = iota((count, rows), 1)
    picks = [sum(jnp.where(at == place + h * cap, 1.0, 0.0) for place in places) for h in range(2)]
    pick = jnp.concatenate(picks, axis=0).astype(BF16)
    for part in range(2):
        found = mm(pick, back_ref[part]).astype(BF16)
        for h in range(2):
            lo = (2 * part + h) * width
            out_ref[:, lo : lo + width] = found[h * count : (h + 1) * count]


def split_width(tokens, out_grad, route_gates, route_slot, gate_weight, up_weight, down_weight):
    count, width = tokens.shape
    top = route_slot.shape[1]
    peers = lax.axis_size("expert")
    planes = peers // PLANE
    cap = capacity_of(count, top, peers)
    w_gate, w_up, w_down = gate_weight[0], up_weight[0], down_weight[0]
    half, ff = w_gate.shape
    quarter = half // 2
    rows = peers * cap
    swap = [(0, 1), (1, 0)]
    index = lax.axis_index("dp").astype(I32)
    group, expert = index.reshape(1), lax.axis_index("expert").astype(I32).reshape(1)
    slots_t = route_slot.T
    place = jnp.arange(rows, dtype=I32)
    straight_left = (place // cap) * (2 * cap) + place % cap
    straight = jnp.concatenate([straight_left, straight_left + cap])
    near, far = masks_of(place // cap, expert)
    moved_left = (far * PLANE + near) * (2 * cap) + place % cap
    moved = jnp.concatenate([moved_left, moved_left + cap])
    tile, narrow = min(256, ff), min(256, half)
    matmul_flops = 2 * 2 * rows * half * ff
    route_flops = 2 * 2 * rows * 2 * count * half
    route_bytes = 2 * (tokens.size + 2 * rows * half)
    weight_bytes = 2 * half * ff

    def shape(*dims, dtype=BF16):
        return jax.ShapeDtypeStruct(dims, dtype)

    near_block, far_block = (planes, 2 * cap, half), (PLANE, 2 * cap, half)

    def exchange(blocks, stride):
        return [blocks[0]] + [
            lax.ppermute(blocks[m], "expert", [(i, i ^ (m * stride)) for i in range(peers)])
            for m in range(1, len(blocks))
        ]

    def regroup(blocks, hold=0):
        outs, *rest = blocks[0].shape
        return call(
            functools.partial(regroup_kernel, len(blocks)),
            tuple(pltpu.HBM((len(blocks), *rest), BF16) for _ in range(outs)),
            (1,),
            [whole(blocks[0].shape)] * len(blocks),
            tuple(whole((len(blocks), *rest)) for _ in range(outs)),
            flops=hold,
            moved=8 * rows * half,
        )(*blocks)

    pieces = 4
    down_halves = call(
        functools.partial(halve_kernel, pieces),
        tuple(pltpu.HBM((quarter, ff), BF16) for _ in range(2)),
        (1,),
        [HBM],
        (HBM, HBM),
        [pltpu.VMEM((half, ff), BF16), pltpu.SemaphoreType.DMA((2, 2, pieces))],
        moved=2 * weight_bytes,
    )(pltpu.with_memory_space_constraint(w_down, pltpu.HBM))
    down_others = [lax.ppermute(each, "dp", swap) for each in down_halves]
    dy_near = call(
        functools.partial(send_grads_kernel, peers, cap),
        tuple(shape(*near_block) for _ in range(PLANE)),
        (1,),
        [SCALAR, SCALAR, whole(slots_t.shape), whole(route_gates.shape), whole(out_grad.shape)],
        tuple(whole(near_block) for _ in range(PLANE)),
        flops=top * route_flops,
        moved=route_bytes,
    )(group, expert, slots_t, route_gates, out_grad)
    dy_far = regroup(exchange(dy_near, 1))

    tok_send = call(
        functools.partial(send_tokens_kernel, peers, cap),
        shape(2, 2 * rows, quarter),
        (1,),
        [whole(slots_t.shape), whole(tokens.shape)],
        whole((2, 2 * rows, quarter)),
        flops=route_flops,
        moved=route_bytes,
    )(slots_t, tokens)
    tok_recv = lax.all_to_all(
        tok_send.reshape(2 * peers, 2 * cap, quarter), ("dp", "expert"), 0, 0, tiled=True
    ).reshape(2, 2 * rows, quarter)

    part_block = pl.BlockSpec((rows, tile), lambda i: (0, i))
    pair_block = pl.BlockSpec((2, rows, tile), lambda i: (0, 0, i))
    weight_block = pl.BlockSpec((half, tile), lambda i: (0, i))
    quarter_block = pl.BlockSpec((quarter, tile), lambda i: (0, i))
    target, *_ = lax.optimization_barrier((straight[:, None], down_others[0], *dy_far))
    pick = call(
        pick_kernel,
        shape(2 * rows, 2 * rows),
        (1,),
        [whole((2 * rows, 1))],
        whole((2 * rows, 2 * rows)),
        flops=AHEAD_OF_PARTIAL,
        moved=8 * rows * rows,
    )(target)

    def partial(other, dtype, received, hold=0):
        return pl.pallas_call(
            functools.partial(partial_kernel, tile),
            out_shape=shape(2, rows, ff, dtype=dtype),
            grid_spec=pltpu.PrefetchScalarGridSpec(
                num_scalar_prefetch=1,
                grid=(1,),
                in_specs=[
                    whole((2 * rows, 2 * rows)),
                    pl.BlockSpec((1, 2 * rows, quarter), lambda i, g: (other ^ g[0], 0, 0)),
                    HBM,
                    HBM,
                ],
                out_specs=whole((2, rows, ff)),
                scratch_shapes=[
                    pltpu.VMEM((rows, half), BF16),
                    pltpu.VMEM((2, half, ff), BF16),
                    pltpu.SemaphoreType.DMA((2, ff // tile)),
                ],
            ),
            cost_estimate=pl.CostEstimate(
                flops=matmul_flops + hold, bytes_accessed=2 * weight_bytes + 2 * rows * half, transcendentals=0
            ),
            compiler_params=pltpu.CompilerParams(vmem_limit_bytes=24 * 2**20),
        )(
            group,
            pick,
            received,
            pltpu.with_memory_space_constraint(w_gate, pltpu.HBM),
            pltpu.with_memory_space_constraint(w_up, pltpu.HBM),
        )

    part_send = partial(1, BF16, tok_recv)
    part_send, down_others[1] = lax.optimization_barrier((part_send, down_others[1]))
    part_recv = lax.ppermute(part_send, "dp", swap)
    dy_came = exchange(dy_far, PLANE)
    part_mine = partial(0, F32, tok_recv)

    d_hidden, dy_mine, dy_other = call(
        hidden_grad_kernel,
        (shape(rows, ff, dtype=F32), shape(rows, half), shape(rows, half)),
        (ff // tile,),
        [whole((2 * rows, 1)), weight_block] + [quarter_block] * 2 + [whole((PLANE * 2 * cap, half))] * planes,
        (part_block, whole((rows, half)), whole((rows, half))),
        [pltpu.VMEM((2 * rows, half), BF16)],
        flops=matmul_flops + AHEAD_OF_BACKWARD,
        moved=2 * weight_bytes + 4 * rows * half,
    )(moved[:, None], w_down, *down_others, *(came.reshape(PLANE * 2 * cap, half) for came in dy_came))
    hidden, d_pair = call(
        pointwise_kernel,
        (shape(rows, ff), shape(2, rows, ff)),
        (ff // tile,),
        [pair_block, pair_block, part_block],
        (part_block, pair_block),
        flops=20 * rows * ff,
        moved=22 * rows * ff,
    )(part_mine, part_recv, d_hidden)
    y_far = call(
        forward_kernel,
        tuple(shape(*far_block) for _ in range(planes)),
        (1,),
        [whole((1, 2 * rows)), whole((rows, ff)), whole((half, ff))] + [whole((quarter, ff))] * 2,
        tuple(whole(far_block) for _ in range(planes)),
        [pltpu.VMEM((2 * rows, quarter), BF16)],
        flops=matmul_flops,
        moved=2 * weight_bytes + 4 * rows * half,
    )(moved[None, :], hidden, w_down, *down_others)
    hidden_recv = lax.ppermute(hidden, "dp", swap)
    d_recv = lax.ppermute(d_pair, "dp", swap)
    dy_other, _ = lax.optimization_barrier((dy_other, d_pair))
    dy_cross = lax.ppermute(dy_other, "dp", swap)

    *_, d_recv = lax.optimization_barrier((*y_far, d_recv))
    y_far_came = exchange(y_far, PLANE)
    def input_grad(other, d_rows, *before):
        return pl.pallas_call(
            functools.partial(input_grad_kernel, other),
            out_shape=shape(2, 2 * rows, quarter),
            grid_spec=pltpu.PrefetchScalarGridSpec(
                num_scalar_prefetch=1,
                grid=(1,),
                in_specs=[
                    whole((1, 2 * rows)),
                    whole((2, rows, ff)),
                    whole((half, ff)),
                    whole((half, ff)),
                    *[HBM for _ in before],
                ],
                out_specs=pl.BlockSpec((1, 2 * rows, quarter), lambda i, g: (other ^ g[0], 0, 0)),
                scratch_shapes=[pltpu.VMEM((2 * rows, quarter), BF16)],
            ),
            input_output_aliases={5: 0} if before else {},
            cost_estimate=pl.CostEstimate(
                flops=matmul_flops, bytes_accessed=2 * weight_bytes + 2 * rows * half, transcendentals=0
            ),
            compiler_params=pltpu.CompilerParams(vmem_limit_bytes=24 * 2**20),
        )(group, straight[None, :], d_rows, w_gate, w_up, *before)

    dx_send = input_grad(1, d_recv, input_grad(0, d_pair))
    y_far_done = y_far_came
    _, *y_far_came = lax.optimization_barrier((dy_cross, *y_far_came))
    y_near = regroup(y_far_came, AHEAD_OF_REGROUP)
    dx_send, *_ = lax.optimization_barrier((dx_send, y_far_done[2]))
    y_came = exchange(y_near, 1)
    dx_back = lax.all_to_all(
        dx_send.reshape(2 * peers, 2 * cap, quarter), ("dp", "expert"), 0, 0, tiled=True
    ).reshape(2, 2 * rows, quarter)

    strip_block = pl.BlockSpec((rows, narrow), lambda i: (0, i))
    down_grad = call(
        down_kernel,
        shape(half, ff),
        (half // narrow,),
        [strip_block, strip_block, whole((rows, ff)), whole((rows, ff))],
        pl.BlockSpec((narrow, ff), lambda i: (i, 0)),
        flops=matmul_flops,
        moved=weight_bytes + 4 * rows * half,
    )(dy_mine, dy_cross, hidden, hidden_recv)[None]
    moe_out = call(
        functools.partial(combine_out_kernel, peers, cap),
        shape(count, width),
        (1,),
        [SCALAR, SCALAR, whole(route_slot.shape), whole(route_gates.shape)]
        + [whole((planes * 2 * cap, half))] * PLANE,
        whole((count, width)),
        [pltpu.VMEM((2 * rows, half), BF16)],
        flops=top * route_flops,
        moved=route_bytes,
    )(group, expert, route_slot, route_gates, *(came.reshape(planes * 2 * cap, half) for came in y_came))
    token_grad = call(
        functools.partial(combine_grad_kernel, peers, cap),
        shape(count, width),
        (1,),
        [whole(route_slot.shape), whole((2, 2 * rows, quarter))],
        whole((count, width)),
        flops=route_flops,
        moved=route_bytes,
    )(route_slot, dx_back)
    return (moe_out, token_grad, down_grad)


def capacity_of(count, top, peers):
    return max(2, (5 * count * top + 4 * peers - 1) // (4 * peers))


def expert_forward(rows_in, w_gate, w_up, w_down):
    gate_proj = jnp.dot(rows_in, w_gate, preferred_element_type=jnp.float32)
    up_proj = jnp.dot(rows_in, w_up, preferred_element_type=jnp.float32)
    sigma_gate = jax.nn.sigmoid(gate_proj)
    activated = gate_proj * sigma_gate
    hidden = (activated * up_proj).astype(jnp.bfloat16)
    outputs = lax.dot_general(
        hidden, w_down, (((1,), (1,)), ((), ())), preferred_element_type=jnp.float32
    ).astype(jnp.bfloat16)
    return (outputs, gate_proj, up_proj, hidden)


def expert_backward(rows_grad, gate_proj, up_proj, w_gate, w_up, w_down):
    grad_hidden = jnp.dot(rows_grad, w_down, preferred_element_type=jnp.float32)
    sigma_gate = jax.nn.sigmoid(gate_proj)
    activated = gate_proj * sigma_gate
    grad_gate = (
        grad_hidden * up_proj * sigma_gate * (1.0 + gate_proj * (1.0 - sigma_gate))
    ).astype(jnp.bfloat16)
    grad_up = (grad_hidden * activated).astype(jnp.bfloat16)
    contract_dims = (((1,), (1,)), ((), ()))
    summed = lax.dot_general(
        grad_gate, w_gate, contract_dims, preferred_element_type=jnp.float32
    ) + lax.dot_general(grad_up, w_up, contract_dims, preferred_element_type=jnp.float32)
    return summed.astype(jnp.bfloat16)


def gathered_weights(tokens, out_grad, route_gates, route_slot, gate_weight, up_weight, down_weight):
    tok_dev, model_width = tokens.shape
    route_count = route_slot.shape[1]
    peer_count = lax.axis_size("expert")
    capacity = capacity_of(tok_dev, route_count, peer_count)
    route_total = tok_dev * route_count
    send_rows = peer_count * capacity
    flat_slot = route_slot.reshape(-1)
    onehot = (flat_slot[:, None] == jnp.arange(peer_count, dtype=jnp.int32)[None, :]).astype(
        jnp.int32
    )
    slot_rank = jnp.sum((jnp.cumsum(onehot, axis=0) - onehot) * onehot, axis=1)
    send_index = flat_slot * capacity + slot_rank
    route_of_row = (
        jnp.full((send_rows,), route_total, jnp.int32)
        .at[send_index]
        .set(jnp.arange(route_total, dtype=jnp.int32))
    )
    filled = route_of_row < route_total
    safe_route = jnp.where(filled, route_of_row, 0)
    token_row = safe_route // route_count
    gate_value = jnp.where(filled, route_gates.reshape(-1)[safe_route], 0.0)
    rows_in = jnp.where(filled[:, None], tokens[token_row], jnp.zeros((), tokens.dtype))
    rows_in = rows_in.reshape(peer_count, capacity, model_width)
    rows_grad = (gate_value[:, None] * out_grad[token_row].astype(jnp.float32)).astype(jnp.bfloat16)
    rows_grad = rows_grad.reshape(peer_count, capacity, model_width)
    full_gate, full_up, full_down = (
        lax.all_gather(gate_weight, "dp", axis=1, tiled=True),
        lax.all_gather(up_weight, "dp", axis=1, tiled=True),
        lax.all_gather(down_weight, "dp", axis=1, tiled=True),
    )
    w_gate = full_gate[0]
    w_up = full_up[0]
    w_down = full_down[0]
    item_shape = (peer_count, capacity, model_width)
    received = lax.all_to_all(rows_in, "expert", split_axis=0, concat_axis=0, tiled=True)
    outputs, gate_proj, up_proj, hidden_saved = expert_forward(
        received.reshape(-1, model_width), w_gate, w_up, w_down
    )
    out_back = lax.all_to_all(
        outputs.reshape(item_shape), "expert", split_axis=0, concat_axis=0, tiled=True
    )
    grad_in = lax.all_to_all(rows_grad, "expert", split_axis=0, concat_axis=0, tiled=True)
    grad_rows = expert_backward(
        grad_in.reshape(-1, model_width), gate_proj, up_proj, w_gate, w_up, w_down
    )
    grad_back = lax.all_to_all(
        grad_rows.reshape(item_shape), "expert", split_axis=0, concat_axis=0, tiled=True
    )
    grad_flat = grad_in.reshape(-1, model_width)
    down_share = lax.psum_scatter(
        lax.dot_general(
            grad_flat, hidden_saved, (((0,), (0,)), ((), ())), preferred_element_type=jnp.float32
        ).astype(jnp.bfloat16),
        "dp",
        scatter_dimension=0,
        tiled=True,
    )
    down_grad = down_share[None]
    out_routes = out_back.reshape(send_rows, model_width)[send_index].astype(jnp.float32)
    out_routes = out_routes.reshape(tok_dev, route_count, model_width)
    moe_out = jnp.sum(route_gates[:, :, None] * out_routes, axis=1).astype(jnp.bfloat16)
    grad_routes = grad_back.reshape(send_rows, model_width)[send_index].astype(jnp.float32)
    token_grad = jnp.sum(grad_routes.reshape(tok_dev, route_count, model_width), axis=1).astype(
        jnp.bfloat16
    )
    return (moe_out, token_grad, down_grad)


def per_device(tokens, out_grad, route_gates, route_slot, gate_weight, up_weight, down_weight):
    count, _ = tokens.shape
    peers = lax.axis_size("expert")
    cap = capacity_of(count, route_slot.shape[1], peers)
    half, hidden_width = gate_weight.shape[1:]
    fits = (
        lax.axis_size("dp") == 2
        and peers % PLANE == 0
        and peers & (peers - 1) == 0
        and cap % 4 == 0
        and (peers * cap) % 16 == 0
        and count % 128 == 0
        and half % 512 == 0
        and hidden_width % 256 == 0
    )
    plan = split_width if fits else gathered_weights
    return plan(tokens, out_grad, route_gates, route_slot, gate_weight, up_weight, down_weight)


def solution(mesh):
    placed = (
        P(("dp", "expert"), None),
        P(("dp", "expert"), None),
        P(("dp", "expert"), None),
        P(("dp", "expert"), None),
        P("expert", "dp", None),
        P("expert", "dp", None),
        P("expert", "dp", None),
    )
    return jax.shard_map(
        per_device,
        mesh=mesh,
        in_specs=placed,
        out_specs=(P(("dp", "expert"), None), P(("dp", "expert"), None), P("expert", "dp", None)),
        check_vma=False,
    )
```
